256 devices in a mesh: section: 4 (over y), group: 8 (over x, core), local: 8 (over z).
Axes of the slice: x: 4, y: 4, z: 8, core: 2. Of those that a mesh axis runs over, the one named last changes fastest.
Arguments:
- hidden_in: bfloat16 [4, 4096, 7168], P('section', ('group', 'local')), may hold values from -6 to 6
- norm_gain: bfloat16 [4, 7168], P('section'), may hold values from 0.099609375 to 1.8984375
- router: bfloat16 [4, 7168, 8], P('section'), may hold values from -0.0625 to 0.0625
- w_gate: bfloat16 [4, 8, 7168, 2048], P('section', 'group', None, 'local'), may hold values from -0.0625 to 0.0625
- w_up: bfloat16 [4, 8, 7168, 2048], P('section', 'group', None, 'local'), may hold values from -0.0625 to 0.0625
- w_down: bfloat16 [4, 8, 2048, 7168], P('section', 'group', 'local'), may hold values from -0.125 to 0.125
- routes: int32 [4, 4096, 2], P('section', ('group', 'local')), may hold values from 0 to 7, all different within a row; in each aligned block of 64 rows (0 to 63, 64 to 127, ..., all dimensions but the last counted through in order) at most 24 rows name the same one
Outputs:
- hidden_out: bfloat16 [4, 4096, 7168], P('section', ('group', 'local'))
The draws below stay inside these ranges and needn't reach their ends.
Inputs may be any that keep to these rules, and one draw needn't show every extreme that they name: `routes`: each token names 2 different experts. Among the 64 tokens of one device (aligned blocks of tokens of one section), no expert is named more than 24 times, and in some blocks one expert is named exactly 24 times.
All inputs are finite; a program needn't handle non-finite values.
Results may differ from the reference program's by a relative error of at most 0.013.
Values may be sent and summed in bfloat16 or wider, within the bound.
A program may use at most 128 MiB of HBM per device.

```python
import math
import jax
import jax.numpy as jnp
import numpy as np
from jax import lax

D = 7168
HID = 2048
TOPK = 2
TOK_DEV = 64
SECTIONS = 4
EXPERTS = 8
HID_DEV = 256
TOKENS = 4096
CAP = 24
N_LOCAL = 8


def levels(stream_key, extent, pieces, smallest, high):
    factor_of = 1.0
    for dim, blocks in pieces:
        steps = jax.random.uniform(jax.random.fold_in(jax.random.fold_in(stream_key, 6), dim), (blocks,), jnp.float32, smallest / len(pieces), high / len(pieces))
        factor_of = factor_of * jnp.repeat(jnp.exp(steps), extent[dim] // blocks).reshape((-1,) + (1,) * (len(extent) - 1 - dim))
    return factor_of


def shared_out(rng, own, number, rows, amount, top, bound, skew):
    sequence = jax.random.permutation(rng, amount)
    crowded, usual = portions_of(amount, rows * top, bound, skew, True), portions_of(amount, rows * top, bound, skew, False)
    places = jnp.arange(amount)

    def named(sizes, rotation):
        used = int((sizes > 0).sum())
        fixed = max(1, used // 4)
        shifted = fixed + (places - fixed + rotation * (used - fixed)) % max(1, amount - fixed)
        return jnp.zeros((amount,), jnp.int32).at[sequence[jnp.where(places < fixed, places, shifted)]].set(jnp.asarray(sizes, jnp.int32))

    sizes = jnp.where(number % 4 == 0, named(crowded, number // 4), named(usual, number - number // 4 - 1))
    mixed = jax.random.permutation(jax.random.fold_in(own, 3), amount)
    source_of, receiver = mixed[0:amount // 2 * 2:2], mixed[1:amount // 2 * 2:2]
    margin = jnp.minimum(sizes[source_of] - 1, bound - sizes[receiver]) // 2
    margin = jnp.where((source_of == sequence[0]) | (receiver == sequence[0]) | (sizes[receiver] == 0), 0, jnp.maximum(margin, 0))
    shifted = jax.random.randint(jax.random.fold_in(own, 4), (amount // 2,), 0, 1 << 20) % (margin + 1)
    sizes = sizes.at[source_of].add(-shifted).at[receiver].add(shifted)
    items = jnp.searchsorted(jnp.cumsum(sizes), jnp.arange(rows * top), side="right").astype(jnp.int32)
    listing = items.reshape(top, rows).T
    listing = listing[jax.random.permutation(jax.random.fold_in(own, 1), rows)]
    rotation = jax.random.randint(jax.random.fold_in(own, 2), (rows, 1), 0, top)
    return jnp.take_along_axis(listing, (jnp.arange(top)[None, :] + rotation) % top, axis=1)


def portions_of(amount, total, limit, lean, full):
    loads = [(1 << 20) // math.isqrt(grade ** lean) + 1 for grade in range(1, amount + 1)]
    largest = limit if full else min(limit, max(-(-total // amount), total * loads[0] // sum(loads)))
    least = 1 if total - largest >= amount - 1 else 0
    counts, rest = [largest] + [least] * (amount - 1), total - largest - least * (amount - 1)
    while rest > 0:
        movable = [i for i in range(1, amount) if counts[i] < largest] or [i for i in range(1, amount) if counts[i] < limit]
        pool, budget = sum([loads[i] for i in movable]), rest
        for i in movable:
            more = min(limit - counts[i], max(1, budget * loads[i] // pool), rest)
            counts[i] = counts[i] + more
            rest = rest - more
    return np.array(counts)


def gaussian(stream_key, dims, spread, most, split=(), kind=jnp.bfloat16):
    array = jax.random.normal(stream_key, dims, jnp.float32) * spread
    if len(split) > 0:
        array = levels(stream_key, dims, split, -0.22, 0.18) * array
    return jnp.clip(array, min=-most, max=most).astype(kind)


def setup_inputs(seed: int = 0) -> dict:
    splits = jax.random.split(jax.random.key(seed), 8)
    hidden_in = gaussian(splits[0], (SECTIONS, TOKENS, D), 1.0, 6.0, ((0, 4), (1, 64)))
    norm_gain = jnp.clip(1.0 + 0.18 * jax.random.normal(splits[1], (SECTIONS, D), jnp.float32), 0.099609375, 1.8984375).astype(jnp.bfloat16)
    router = gaussian(splits[2], (SECTIONS, D, EXPERTS), D ** -0.5, 0.0625, ((0, 4),))
    w_gate = gaussian(splits[3], (SECTIONS, EXPERTS, D, HID), D ** -0.5, 0.0625, ((0, 4), (1, 8), (3, 8)))
    w_up = gaussian(splits[4], (SECTIONS, EXPERTS, D, HID), D ** -0.5, 0.0625, ((0, 4), (1, 8), (3, 8)))
    w_down = gaussian(splits[5], (SECTIONS, EXPERTS, HID, D), HID ** -0.5, 0.125, ((0, 4), (1, 8), (2, 8)))
    routes_keys = jax.random.split(jax.random.fold_in(splits[6], 1), SECTIONS * TOKENS // TOK_DEV)
    routes_turns = jax.random.permutation(jax.random.fold_in(splits[6], 3), SECTIONS * TOKENS // TOK_DEV)
    routes = jax.vmap(lambda own, number: shared_out(jax.random.fold_in(splits[6], 2), own, number, TOK_DEV, EXPERTS, TOPK, CAP, 2))(routes_keys, routes_turns).reshape((SECTIONS, TOKENS, TOPK))
    return dict(hidden_in=hidden_in, norm_gain=norm_gain, router=router, w_gate=w_gate, w_up=w_up, w_down=w_down, routes=routes)


def norm_rows(incoming, gain_row):
    values = incoming.astype(jnp.float32)
    meansq = lax.optimization_barrier(jnp.mean(values * values, axis=-1, keepdims=True))
    return (values * lax.rsqrt(meansq + 1e-06) * gain_row.astype(jnp.float32)).astype(jnp.bfloat16)

def route_gates(normed, router_matrix, choices_ids):
    logits = jnp.dot(normed, router_matrix, preferred_element_type=jnp.float32)
    affinity = jax.nn.sigmoid(logits)
    picked = jnp.take_along_axis(affinity, choices_ids, axis=1)
    return 2.5 * picked / lax.optimization_barrier(jnp.sum(picked, axis=1, keepdims=True))

def slot_numbers(route_blocks, experts_total):
    onehot = (route_blocks[..., None] == jnp.arange(experts_total, dtype=jnp.int32)).astype(jnp.int32)
    earlier = jnp.cumsum(onehot, axis=-2) - onehot
    return lax.optimization_barrier(jnp.sum(earlier * onehot, axis=-1))

def section_layer(incoming, gain_row, router_matrix, gate_stack, up_stack, down_stack, choices_ids):
    normed = norm_rows(incoming, gain_row)
    gate_weights = route_gates(normed, router_matrix, choices_ids)
    devices = TOKENS // TOK_DEV
    local_slot = slot_numbers(choices_ids.reshape(devices, TOK_DEV * TOPK), EXPERTS)
    owner_base = jnp.arange(devices, dtype=jnp.int32)[:, None] * CAP
    slot_index = (owner_base + local_slot).reshape(TOKENS, TOPK).astype(jnp.int32)
    token_index = jnp.broadcast_to(jnp.arange(TOKENS, dtype=jnp.int32)[:, None], (TOKENS, TOPK))
    slot_table = jnp.full((EXPERTS, devices * CAP), TOKENS, jnp.int32)
    slot_table = slot_table.at[choices_ids.reshape(-1), slot_index.reshape(-1)].set(token_index.reshape(-1))
    padded = jnp.concatenate([normed, jnp.zeros((1, D), jnp.bfloat16)], axis=0)

    def run_expert(expert_id):
        slot_rows = padded[slot_table[expert_id]]
        gate_part = jnp.dot(slot_rows, gate_stack[expert_id], preferred_element_type=jnp.float32)
        up_part = jnp.dot(slot_rows, up_stack[expert_id], preferred_element_type=jnp.float32)
        active = (jax.nn.silu(gate_part) * up_part).astype(jnp.bfloat16)
        summed = jnp.zeros((devices * CAP, D), jnp.float32)
        for piece in range(N_LOCAL):
            offset = piece * HID_DEV
            partial_value = jnp.dot(active[:, offset:offset + HID_DEV], down_stack[expert_id, offset:offset + HID_DEV], preferred_element_type=jnp.float32).astype(jnp.bfloat16)
            summed = summed + lax.optimization_barrier(partial_value).astype(jnp.float32)
        return summed.astype(jnp.bfloat16)
    outputs = lax.map(run_expert, jnp.arange(EXPERTS, dtype=jnp.int32))
    routed = outputs[choices_ids, slot_index].astype(jnp.float32)
    mixed_rows = incoming.astype(jnp.float32) + lax.optimization_barrier(jnp.sum(gate_weights[..., None] * routed, axis=1))
    return mixed_rows.astype(jnp.bfloat16)

def reference(hidden_in, norm_gain, router, w_gate, w_up, w_down, routes):
    incoming = jnp.roll(hidden_in, 1, axis=0)
    results = []
    for section_id in range(SECTIONS):
        results.append(section_layer(incoming[section_id], norm_gain[section_id], router[section_id], w_gate[section_id], w_up[section_id], w_down[section_id], routes[section_id]))
    return jnp.stack(results)
```

```python
import functools

import jax
import jax.numpy as jnp
from jax import lax
from jax.experimental import pallas as pl
from jax.experimental.pallas import tpu as pltpu
from jax.sharding import PartitionSpec as P

WIDTH = 7168
WIDTH_A = 3840
WIDTH_B = WIDTH - WIDTH_A
META = 128
WIDTH_BX = WIDTH_B + META
EXPERTS = 8
LOCALS = 8
ROWS = 64
CAP = 24
PAD = 32
SLOTS = EXPERTS * CAP
PAIRS = LOCALS // 2
HALF = 256
VMEM_BYTES = 63 * 2**20

BF16 = jnp.bfloat16
F32 = jnp.float32


def wrap(value, count=8):
    return lax.rem(value + 2 * count, count)


def spans(width, pieces):
    tiles = width // 128
    cuts = [128 * (tiles * i // pieces) for i in range(pieces + 1)]
    return [(cuts[i], cuts[i + 1] - cuts[i]) for i in range(pieces)]


def matmul(left, right):
    return jnp.dot(left, right, preferred_element_type=F32)


def enter(group, local):
    barrier = pltpu.get_barrier_semaphore()
    for step in (1, 7):
        pl.semaphore_signal(barrier, inc=1, device_id={"local": wrap(local + step)})
    for step in range(1, EXPERTS):
        pl.semaphore_signal(barrier, inc=1, device_id={"group": wrap(group + step)})
    pl.semaphore_wait(barrier, 2 + EXPERTS - 1)


def remote(src, dst, send, recv, device):
    return pltpu.make_async_remote_copy(
        src_ref=src, dst_ref=dst, send_sem=send, recv_sem=recv, device_id=device
    )


def hops_of(piece, pieces, way):
    first = piece < pieces // 2
    return 4 if first == (way == 0) else 3


def slot_masks(meta, columns, slot_of, expert_of, extra):
    out = []
    for choice in range(2):
        expert = meta[:, 2 * choice : 2 * choice + 1]
        slot = meta[:, 2 * choice + 1 : 2 * choice + 2]
        hit = (expert_of == expert) & (slot_of == slot)
        if extra is not None:
            hit = hit & extra
        out.append(hit)
    return out


def dispatch_kernel(
    disp_ref, tok_ref, wg_ref, wu_ref, acta_ref, actb_ref, meta_ref,
    xa, za, zb, xs, xr, hacc,
    xa_send, xa_recv, zb_send, zb_recv, za_send, za_recv, xb_send, xb_recv,
):
    group, local = lax.axis_index("group"), lax.axis_index("local")
    ring = ({"local": wrap(local + 1)}, {"local": wrap(local - 1)})
    sign = (1, -1)
    cuts_a, cuts_b = spans(WIDTH_A, 4), spans(WIDTH_BX, 2)
    enter(group, local)
    sent = []

    def start(copy):
        copy.start()
        sent.append(copy)

    def ring_copy(buffer, sends, recvs, cuts, way, hop, piece, src=None):
        begin, size = cuts[piece]
        block = wrap(local - sign[way] * (hop - 1))
        columns = pl.ds(begin, size)
        view = buffer.at[block, :, columns]
        return remote(
            view if src is None else src.at[:, columns],
            view,
            sends.at[way, hop - 1, piece],
            recvs.at[way, hop - 1, piece],
            ring[way],
        )

    def ring_step(buffer, sends, recvs, cuts, hop):
        for piece in range(len(cuts)):
            for way in range(2):
                hops = hops_of(piece, len(cuts), way)
                if hop <= hops:
                    ring_copy(buffer, sends, recvs, cuts, way, hop, piece).wait_recv()
                if hop < hops:
                    start(ring_copy(buffer, sends, recvs, cuts, way, hop + 1, piece))

    for piece in range(2):
        for way in range(2):
            start(ring_copy(zb, zb_send, zb_recv, cuts_b, way, 1, piece, tok_ref))
    xa_copies = []
    for step in range(1, EXPERTS):
        other = wrap(group + step)
        copy = remote(
            disp_ref.at[other], xa.at[group], xa_send.at[step], xa_recv.at[step], {"group": other}
        )
        start(copy)
        xa_copies.append(copy)
    zb[local] = tok_ref[...]
    xa[group] = disp_ref[group]

    ring_step(zb, zb_send, zb_recv, cuts_b, 1)
    ring_step(zb, zb_send, zb_recv, cuts_b, 2)
    ring_step(zb, zb_send, zb_recv, cuts_b, 3)
    for copy in xa_copies:
        copy.wait_recv()

    @pl.loop(0, WIDTH_A // HALF)
    def _(tile):
        columns = pl.ds(pl.multiple_of(tile * HALF, HALF), HALF)
        rows = xa[:, :, columns].astype(F32)
        za[local, :, columns] = rows[:, :CAP].reshape(SLOTS, HALF).astype(BF16)

    for piece in range(4):
        for way in range(2):
            start(ring_copy(za, za_send, za_recv, cuts_a, way, 1, piece))
    ring_step(zb, zb_send, zb_recv, cuts_b, 4)

    @pl.loop(0, PAIRS)
    def _(pair):
        meta = zb[pl.ds(2 * pair, 2), :, pl.ds(WIDTH_B, META)].reshape(2 * ROWS, META)
        meta_ref[pl.ds(2 * pair, 2)] = meta.reshape(2, ROWS, META)
        shape = (2 * ROWS, EXPERTS * 2 * CAP)
        column = lax.broadcasted_iota(jnp.int32, shape, 1)
        inside = lax.rem(column, 2 * CAP)
        owner = lax.broadcasted_iota(jnp.int32, shape, 0) // ROWS
        masks = slot_masks(
            meta.astype(F32),
            shape[1],
            lax.rem(inside, CAP).astype(F32),
            (column // (2 * CAP)).astype(F32),
            inside // CAP == owner,
        )
        selector = jnp.transpose((masks[0] | masks[1]).astype(F32)).astype(BF16)

        @pl.loop(0, WIDTH_B // HALF)
        def _(tile):
            columns = pl.ds(pl.multiple_of(tile * HALF, HALF), HALF)
            rows = zb[pl.ds(2 * pair, 2), :, columns].reshape(2 * ROWS, HALF)
            picked = matmul(selector, rows).astype(BF16).reshape(EXPERTS, 2 * CAP, HALF)
            xs[:, pl.ds(pl.multiple_of(pair * 2 * CAP, 2 * CAP), 2 * CAP), columns] = picked

    xb_copies = []
    for step in range(1, EXPERTS):
        other = wrap(group + step)
        copy = remote(xs.at[other], xr.at[group], xb_send.at[step], xb_recv.at[step], {"group": other})
        start(copy)
        xb_copies.append(copy)

    def add_a(block, _):
        block = wrap(block)
        rows = za[block]
        for half, weights in enumerate((wg_ref, wu_ref)):
            out = matmul(rows, weights[:WIDTH_A, :]).reshape(EXPERTS, CAP, HALF)
            hacc[block, :, :, half * HALF : (half + 1) * HALF] = out
        return _

    def add_b(source, owner):
        rows = source[owner]
        for half, weights in enumerate((wg_ref, wu_ref)):
            out = matmul(rows, weights[WIDTH_A:, :]).reshape(LOCALS, CAP, HALF)
            hacc[:, owner, :, half * HALF : (half + 1) * HALF] += out

    lax.fori_loop(local, local + 1, add_a, 0)
    for hop in range(1, 4):
        ring_step(za, za_send, za_recv, cuts_a, hop)
        lax.fori_loop(0, 2, lambda i, c, hop=hop: add_a(local - hop + 2 * hop * i, c), 0)
    ring_step(za, za_send, za_recv, cuts_a, 4)
    lax.fori_loop(local + 4, local + 5, add_a, 0)
    add_b(xs, group)
    for copy in xb_copies:
        copy.wait_recv()

    @pl.loop(1, EXPERTS)
    def _(step):
        add_b(xr, wrap(group - step))

    @pl.loop(0, LOCALS)
    def _(block):
        gate = hacc[block, :, :, :HALF]
        up = hacc[block, :, :, HALF:]
        active = jax.nn.silu(gate) * up
        hacc[block, :, :, :HALF] = active
        acta_ref[block] = active.reshape(SLOTS, HALF).astype(BF16)

    @pl.loop(0, EXPERTS)
    def _(owner):
        actb_ref[owner] = hacc[:, owner, :, :HALF].reshape(SLOTS, HALF).astype(BF16)

    for copy in sent:
        copy.wait_send()


def combine_kernel(
    acta_ref, actb_ref, wd_ref, meta_ref, inc_ref, out_ref,
    za, ru, rd, xs, xr, tb, tu, td, sb, ra,
    xb_send, xb_recv, za_send, za_recv, zb_send, zb_recv, xa_send, xa_recv,
):
    group, local = lax.axis_index("group"), lax.axis_index("local")
    ring = ({"local": wrap(local + 1)}, {"local": wrap(local - 1)})
    sign = (1, -1)
    cuts_a, cuts_b = spans(WIDTH_A, 4), spans(WIDTH_B, 2)
    enter(group, local)
    sent = []

    def start(copy):
        copy.start()
        sent.append(copy)

    def product_a(block):
        @pl.loop(0, WIDTH_A // HALF)
        def _(tile):
            columns = pl.ds(pl.multiple_of(tile * HALF, HALF), HALF)
            za[block, :, columns] = matmul(acta_ref[block], wd_ref[:, columns]).astype(BF16)

    def product_b(target, owner):
        @pl.loop(0, WIDTH_B // HALF)
        def _(tile):
            columns = pl.ds(pl.multiple_of(tile * HALF, HALF), HALF)
            weights = wd_ref[:, pl.ds(pl.multiple_of(WIDTH_A + tile * HALF, HALF), HALF)]
            target[owner, :, columns] = matmul(actb_ref[owner], weights).astype(BF16)

    def ring_copy(buffer, landed, sends, recvs, cuts, way, hop, piece):
        begin, size = cuts[piece]
        block = wrap(local + sign[way] * (5 - hop))
        columns = pl.ds(begin, size)
        return remote(
            buffer.at[block, :, columns],
            landed[way].at[hop - 1, :, columns],
            sends.at[way, hop - 1, piece],
            recvs.at[way, hop - 1, piece],
            ring[way],
        )

    def ring_step(buffer, landed, sends, recvs, cuts, hop):
        for piece in range(len(cuts)):
            for way in range(2):
                first = 5 - hops_of(piece, len(cuts), way)
                if hop < first:
                    continue
                if hop > first:
                    ring_copy(buffer, landed, sends, recvs, cuts, way, hop - 1, piece).wait_recv()
                    begin, size = cuts[piece]
                    columns = pl.ds(begin, size)
                    block = wrap(local + sign[way] * (5 - hop))
                    came = landed[way]
                    buffer[block, :, columns] += came[hop - 2, :, columns]
                start(ring_copy(buffer, landed, sends, recvs, cuts, way, hop, piece))

    ring_a = (za, (ru, rd), za_send, za_recv, cuts_a)
    ring_b = (tb, (tu, td), zb_send, zb_recv, cuts_b)

    product_a(wrap(local + 4))
    ring_step(*ring_a, 1)
    xb_copies = []
    for step in range(1, EXPERTS):
        other = wrap(group + step)
        product_b(xs, other)
        copy = remote(xs.at[other], xr.at[group], xb_send.at[step], xb_recv.at[step], {"group": other})
        start(copy)
        xb_copies.append(copy)
    for distance in (3, 2, 1):
        lax.fori_loop(
            0, 2, lambda i, c, d=distance: (product_a(wrap(local - d + 2 * d * i)), c)[1], 0
        )
        ring_step(*ring_a, 5 - distance)
    product_a(local)
    product_b(xr, group)
    sb[...] = jnp.zeros_like(sb)

    for copy in xb_copies:
        copy.wait_recv()

    @pl.loop(0, PAIRS)
    def _(pair):
        meta = meta_ref[pl.ds(2 * pair, 2)].reshape(2 * ROWS, META).astype(F32)
        shape = (2 * ROWS, EXPERTS * 2 * CAP)
        column = lax.broadcasted_iota(jnp.int32, shape, 1)
        inside = lax.rem(column, 2 * CAP)
        owner = lax.broadcasted_iota(jnp.int32, shape, 0) // ROWS
        masks = slot_masks(
            meta,
            shape[1],
            lax.rem(inside, CAP).astype(F32),
            (column // (2 * CAP)).astype(F32),
            inside // CAP == owner,
        )
        high, low = gate_matrices(meta, masks)

        @pl.loop(0, WIDTH_B // HALF)
        def _(tile):
            columns = pl.ds(pl.multiple_of(tile * HALF, HALF), HALF)
            rows = xr[:, pl.ds(pl.multiple_of(pair * 2 * CAP, 2 * CAP), 2 * CAP), columns]
            rows = rows.reshape(EXPERTS * 2 * CAP, HALF)
            mixed = matmul(high, rows) + matmul(low, rows)
            tb[pl.ds(2 * pair, 2), :, columns] = mixed.astype(BF16).reshape(2, ROWS, HALF)

    ring_step(*ring_b, 1)
    ring_step(*ring_b, 2)
    for piece in range(4):
        for way in range(2):
            ring_copy(*ring_a, way, 4, piece).wait_recv()

    @pl.loop(0, WIDTH_A // HALF)
    def _(tile):
        columns = pl.ds(pl.multiple_of(tile * HALF, HALF), HALF)
        total = (
            za[local, :, columns].astype(F32)
            + ru[3, :, columns].astype(F32)
            + rd[3, :, columns].astype(F32)
        ).reshape(EXPERTS, CAP, HALF)
        gap = jnp.zeros((EXPERTS, PAD - CAP, HALF), F32)
        sb[:, :, columns] = jnp.concatenate([total, gap], axis=1).astype(BF16)

    xa_copies = []
    for step in range(1, EXPERTS):
        other = wrap(group + step)
        copy = remote(sb.at[other], ra.at[group], xa_send.at[step], xa_recv.at[step], {"group": other})
        start(copy)
        xa_copies.append(copy)
    ra[group] = sb[group]
    ring_step(*ring_b, 3)
    ring_step(*ring_b, 4)

    meta = meta_ref[local].astype(F32)
    shape = (ROWS, EXPERTS * PAD)
    column = lax.broadcasted_iota(jnp.int32, shape, 1)
    masks = slot_masks(
        meta, shape[1], lax.rem(column, PAD).astype(F32), (column // PAD).astype(F32), None
    )
    high, low = gate_matrices(meta, masks)
    for copy in xa_copies:
        copy.wait_recv()

    @pl.loop(0, WIDTH_A // HALF)
    def _(tile):
        columns = pl.ds(pl.multiple_of(tile * HALF, HALF), HALF)
        rows = ra[:, :, columns].reshape(EXPERTS * PAD, HALF)
        mixed = matmul(high, rows) + matmul(low, rows)
        out_ref[:, columns] = (inc_ref[:, columns].astype(F32) + mixed).astype(BF16)

    for piece in range(2):
        for way in range(2):
            ring_copy(*ring_b, way, 4, piece).wait_recv()

    @pl.loop(0, WIDTH_B // HALF)
    def _(tile):
        columns = pl.ds(pl.multiple_of(tile * HALF, HALF), HALF)
        places = pl.ds(pl.multiple_of(WIDTH_A + tile * HALF, HALF), HALF)
        mixed = (
            tb[local, :, columns].astype(F32)
            + tu[3, :, columns].astype(F32)
            + td[3, :, columns].astype(F32)
        )
        out_ref[:, places] = (inc_ref[:, places].astype(F32) + mixed).astype(BF16)

    for copy in sent:
        copy.wait_send()


def gate_matrices(meta, masks):
    out = []
    for part in range(2):
        first, second = meta[:, 4 + part : 5 + part], meta[:, 6 + part : 7 + part]
        out.append((jnp.where(masks[0], first, 0.0) + jnp.where(masks[1], second, 0.0)).astype(BF16))
    return out


def norm_rows(incoming, gain_row):
    values = incoming.astype(F32)
    meansq = jnp.mean(values * values, axis=-1, keepdims=True)
    return (values * lax.rsqrt(meansq + 1e-06) * gain_row.astype(F32)).astype(BF16)


def route_gates(normed, router_matrix, choices_ids):
    logits = jnp.dot(normed, router_matrix, preferred_element_type=F32)
    affinity = jax.nn.sigmoid(logits)
    picked = jnp.take_along_axis(affinity, choices_ids, axis=1)
    return 2.5 * picked / jnp.sum(picked, axis=1, keepdims=True)


def slot_numbers(route_blocks, experts_total):
    onehot = (route_blocks[..., None] == jnp.arange(experts_total, dtype=jnp.int32)).astype(jnp.int32)
    earlier = jnp.cumsum(onehot, axis=-2) - onehot
    return jnp.sum(earlier * onehot, axis=-1)


def whole(shape, dtype=BF16):
    return pltpu.VMEM(shape, dtype)


def dma(*shape):
    return pltpu.SemaphoreType.DMA(shape)


def params(number):
    return pltpu.CompilerParams(
        collective_id=number, has_side_effects=True, vmem_limit_bytes=VMEM_BYTES
    )


def per_device(hidden_in, norm_gain, router, w_gate, w_up, w_down, routes):
    count = lax.axis_size("section")
    shifted = lax.ppermute(hidden_in, "section", [(i, (i + 1) % count) for i in range(count)])
    incoming = shifted[0]
    choices = routes[0]
    normed = norm_rows(incoming, norm_gain[0])
    gates = route_gates(normed, router[0], choices)
    slot = slot_numbers(choices.reshape(1, -1), EXPERTS)[0].reshape(ROWS, 2)

    place = choices * PAD + slot
    ids = jnp.arange(EXPERTS * PAD, dtype=jnp.int32)
    selector = jnp.any(ids[:, None, None] == place[None], axis=2).astype(BF16)
    disp = jnp.dot(selector, normed[:, :WIDTH_A], preferred_element_type=F32).astype(BF16)
    disp = disp.reshape(EXPERTS, PAD, WIDTH_A)

    high = gates.astype(BF16)
    low = (gates - high.astype(F32)).astype(BF16)
    meta = [choices[:, :1], slot[:, :1], choices[:, 1:], slot[:, 1:]]
    meta = [m.astype(BF16) for m in meta]
    meta += [high[:, :1], low[:, :1], high[:, 1:], low[:, 1:]]
    meta = jnp.concatenate(meta + [jnp.zeros((ROWS, META - 8), BF16)], axis=1)
    tokens = jnp.concatenate([normed[:, WIDTH_A:], meta], axis=1)

    vmem = pl.BlockSpec(memory_space=pltpu.VMEM)
    acta, actb, metas = pl.pallas_call(
        dispatch_kernel,
        out_shape=(
            jax.ShapeDtypeStruct((LOCALS, SLOTS, HALF), BF16),
            jax.ShapeDtypeStruct((EXPERTS, SLOTS, HALF), BF16),
            jax.ShapeDtypeStruct((LOCALS, ROWS, META), BF16),
        ),
        in_specs=[vmem] * 4,
        out_specs=(vmem,) * 3,
        scratch_shapes=[
            whole((EXPERTS, PAD, WIDTH_A)),
            whole((LOCALS, SLOTS, WIDTH_A)),
            whole((LOCALS, ROWS, WIDTH_BX)),
            whole((EXPERTS, SLOTS, WIDTH_B)),
            whole((EXPERTS, SLOTS, WIDTH_B)),
            whole((LOCALS, EXPERTS, CAP, 2 * HALF), F32),
            dma(8), dma(8), dma(2, 4, 2), dma(2, 4, 2), dma(2, 4, 4), dma(2, 4, 4), dma(8), dma(8),
        ],
        compiler_params=params(0),
        name="dispatch",
    )(disp, tokens, w_gate[0, 0], w_up[0, 0])

    mixed = pl.pallas_call(
        combine_kernel,
        out_shape=jax.ShapeDtypeStruct((ROWS, WIDTH), BF16),
        in_specs=[vmem] * 5,
        out_specs=vmem,
        scratch_shapes=[
            whole((LOCALS, SLOTS, WIDTH_A)),
            whole((4, SLOTS, WIDTH_A)),
            whole((4, SLOTS, WIDTH_A)),
            whole((EXPERTS, SLOTS, WIDTH_B)),
            whole((EXPERTS, SLOTS, WIDTH_B)),
            whole((LOCALS, ROWS, WIDTH_B)),
            whole((4, ROWS, WIDTH_B)),
            whole((4, ROWS, WIDTH_B)),
            whole((EXPERTS, PAD, WIDTH_A)),
            whole((EXPERTS, PAD, WIDTH_A)),
            dma(8), dma(8), dma(2, 4, 4), dma(2, 4, 4), dma(2, 4, 2), dma(2, 4, 2), dma(8), dma(8),
        ],
        compiler_params=params(1),
        name="combine",
    )(acta, actb, w_down[0, 0], metas, incoming)
    return mixed[None]


def solution(mesh):
    placed = (
        P("section", ("group", "local"), None),
        P("section", None),
        P("section", None, None),
        P("section", "group", None, "local"),
        P("section", "group", None, "local"),
        P("section", "group", "local", None),
        P("section", ("group", "local"), None),
    )
    return jax.shard_map(
        per_device,
        mesh=mesh,
        in_specs=placed,
        out_specs=P("section", ("group", "local"), None),
        check_vma=False,
    )
```

```python
import jax
import jax.numpy as jnp
from jax import lax
from jax.experimental import pallas as pl
from jax.experimental.pallas import tpu as pltpu
from jax.sharding import PartitionSpec as P

WIDTH = 7168
WIDTH_A = 3584
HALF_A = WIDTH_A // 2
WIDTH_B = WIDTH - WIDTH_A
META = 128
WIDTH_BX = WIDTH_B + META
EXPERTS = 8
LOCALS = 8
ROWS = 64
CAP = 24
TWICE = 2 * CAP
SLOTS = EXPERTS * CAP
PAIRS = LOCALS // 2
HIDDEN = 256
TILE = 256
CHUNKS = 4
CHUNK = ROWS // CHUNKS
PIECES = 4
VMEM_BYTES = 63 * 2**20

BF16 = jnp.bfloat16
F32 = jnp.float32


def wrap(value, count=8):
    return lax.rem(value + 2 * count, count)


def spans(width, pieces):
    tiles = width // 128
    cuts = [128 * (tiles * i // pieces) for i in range(pieces + 1)]
    return [(cuts[i], cuts[i + 1] - cuts[i]) for i in range(pieces)]


def matmul(left, right):
    return jnp.dot(left, right, preferred_element_type=F32)


def tile_at(tile, base=0):
    return pl.ds(pl.multiple_of(base + tile * TILE, TILE), TILE)


def pair_at(pair):
    return pl.ds(pl.multiple_of(pair * TWICE, TWICE), TWICE)


def remote(src, dst, send, recv, device):
    return pltpu.make_async_remote_copy(
        src_ref=src, dst_ref=dst, send_sem=send, recv_sem=recv, device_id=device
    )


def hops_of(piece, pieces, way):
    first = piece < pieces // 2
    return 4 if first == (way == 0) else 3


def pairs_near_first(local):
    own = local // 2
    odd = lax.rem(local, 2)
    return [own, wrap(own + 2 * odd - 1, PAIRS), wrap(own - 2 * odd + 1, PAIRS), wrap(own + 2, PAIRS)]


def slot_masks(meta, expert_of, slot_of):
    out = []
    for choice in range(2):
        expert = meta[:, 2 * choice : 2 * choice + 1]
        slot = meta[:, 2 * choice + 1 : 2 * choice + 2]
        out.append((expert_of == expert) & (slot_of == slot))
    return out


def pair_masks(meta):
    shape = (2 * ROWS, EXPERTS * TWICE)
    column = lax.broadcasted_iota(jnp.int32, shape, 1)
    inside = lax.rem(column, TWICE)
    owner = lax.broadcasted_iota(jnp.int32, shape, 0) // ROWS
    slot = jnp.where(inside // CAP == owner, lax.rem(inside, CAP), -1)
    return slot_masks(meta, (column // TWICE).astype(F32), slot.astype(F32))


def gate_matrices(meta):
    masks = pair_masks(meta)
    out = []
    for part in range(2):
        first, second = meta[:, 4 + part : 5 + part], meta[:, 6 + part : 7 + part]
        out.append((jnp.where(masks[0], first, 0.0) + jnp.where(masks[1], second, 0.0)).astype(BF16))
    return out


def dispatch_kernel(
    hid_ref, gain_ref, router_ref, routes_ref, wg_ref, wu_ref,
    acta_ref, actb_ref, meta_ref, inc_ref,
    inc, na, disp, xa, za, zb, xs, xr, hacc,
    y_send, y_recv, xa_send, xa_recv, zb_send, zb_recv, za_send, za_recv, xb_send, xb_recv,
):
    section = lax.axis_index("section")
    group, local = lax.axis_index("group"), lax.axis_index("local")
    ring = ({"local": wrap(local + 1)}, {"local": wrap(local - 1)})
    sign = (1, -1)
    cuts_a = spans(WIDTH_A, PIECES)
    pairs = pairs_near_first(local)
    sent = []

    barrier = pltpu.get_barrier_semaphore()
    pl.semaphore_signal(barrier, inc=1, device_id={"section": wrap(section - 1, 4)})
    for step in (1, 7):
        pl.semaphore_signal(barrier, inc=1, device_id={"local": wrap(local + step)})
    for step in range(1, EXPERTS):
        pl.semaphore_signal(barrier, inc=1, device_id={"group": wrap(group + step)})
    pl.semaphore_wait(barrier, 1 + 2 + EXPERTS - 1)

    def start(copy):
        copy.start()
        sent.append(copy)
        return copy

    def view_a(block, piece):
        begin, size = cuts_a[piece]
        return za.at[block, :, pl.ds(begin, size)]

    def view_b(block, piece):
        return zb.at[block, pl.ds(piece * CHUNK, CHUNK)]

    def ring_copy(kind, way, hop, piece):
        view, sends, recvs = kind
        there = view(wrap(local - sign[way] * (hop - 1)), piece)
        return remote(
            there, there, sends.at[way, hop - 1, piece], recvs.at[way, hop - 1, piece], ring[way]
        )

    def ring_step(kind, hop):
        for piece in range(4):
            for way in range(2):
                hops = hops_of(piece, 4, way)
                if hop <= hops:
                    ring_copy(kind, way, hop, piece).wait_recv()
                if hop < hops:
                    start(ring_copy(kind, way, hop + 1, piece))

    ring_a = (view_a, za_send, za_recv)
    ring_b = (view_b, zb_send, zb_recv)

    shifts = []
    for chunk in range(CHUNKS):
        rows = pl.ds(chunk * CHUNK, CHUNK)
        shifts.append(
            start(
                remote(
                    hid_ref.at[rows], inc.at[rows], y_send.at[chunk], y_recv.at[chunk],
                    {"section": wrap(section + 1, 4)},
                )
            )
        )

    lane = lax.broadcasted_iota(jnp.int32, (ROWS, META), 1)
    named = [routes_ref[:, choice : choice + 1] == lane for choice in range(2)]
    later = lax.broadcasted_iota(jnp.int32, (ROWS, ROWS), 0)
    earlier = lax.broadcasted_iota(jnp.int32, (ROWS, ROWS), 1)
    counts = (named[0].astype(F32) + named[1].astype(F32)).astype(BF16)
    before = matmul((later > earlier).astype(F32).astype(BF16), counts)
    meta = jnp.zeros((ROWS, META), F32)
    for choice in range(2):
        slot = jnp.sum(jnp.where(named[choice], before, 0.0), axis=1, keepdims=True)
        meta = jnp.where(lane == 2 * choice, routes_ref[:, choice : choice + 1].astype(F32), meta)
        meta = jnp.where(lane == 2 * choice + 1, slot, meta)

    for chunk in range(CHUNKS):
        shifts[chunk].wait_recv()
        rows = pl.ds(chunk * CHUNK, CHUNK)
        raw = inc[rows]
        inc_ref[rows] = raw
        values = raw.astype(F32)
        scale = lax.rsqrt(jnp.mean(values * values, axis=-1, keepdims=True) + 1e-06)
        normed = (values * scale * gain_ref[...].astype(F32)).astype(BF16)
        na[rows] = normed[:, :WIDTH_A]
        zb[local, rows, :WIDTH_B] = normed[:, WIDTH_A:]
        affinity = jax.nn.sigmoid(matmul(normed, router_ref[...]))
        part = meta[chunk * CHUNK : (chunk + 1) * CHUNK]
        expert = lax.broadcasted_iota(jnp.int32, (CHUNK, EXPERTS), 1).astype(F32)
        picked = [
            jnp.sum(
                jnp.where(part[:, 2 * choice : 2 * choice + 1] == expert, affinity, 0.0),
                axis=1,
                keepdims=True,
            )
            for choice in range(2)
        ]
        place = lane[:CHUNK]
        for choice in range(2):
            gate = 2.5 * picked[choice] / (picked[0] + picked[1])
            high = gate.astype(BF16).astype(F32)
            part = jnp.where(place == 4 + 2 * choice, high, part)
            part = jnp.where(place == 5 + 2 * choice, gate - high, part)
        zb[local, rows, WIDTH_B:] = part.astype(BF16)
        for way in range(2):
            start(ring_copy(ring_b, way, 1, chunk))

    column = lax.broadcasted_iota(jnp.int32, (ROWS, EXPERTS * 32), 1)
    masks = slot_masks(meta, (column // 32).astype(F32), lax.rem(column, 32).astype(F32))
    chosen = (masks[0] | masks[1]).astype(F32)
    chosen = jnp.transpose(jnp.concatenate([chosen, jnp.zeros_like(chosen)], axis=0))
    chosen = chosen.reshape(EXPERTS, 32, 2 * ROWS)[:, :CAP].reshape(SLOTS, 2 * ROWS)
    chosen = chosen[:, :ROWS].astype(BF16)

    @pl.loop(0, HALF_A // TILE)
    def _(tile):
        halves = [
            matmul(chosen, na[:, tile_at(tile, base)]).reshape(EXPERTS, CAP, TILE)
            for base in (0, HALF_A)
        ]
        disp[:, :, tile_at(tile)] = jnp.concatenate(halves, axis=1).astype(BF16)

    xa_copies = []
    for step in range(1, EXPERTS):
        other = wrap(group + step)
        copy = remote(
            disp.at[other], xa.at[group], xa_send.at[step], xa_recv.at[step], {"group": other}
        )
        xa_copies.append(start(copy))
    xa[group] = disp[group]

    def select(pair):
        meta = zb[pl.ds(2 * pair, 2), :, pl.ds(WIDTH_B, META)]
        meta_ref[pl.ds(2 * pair, 2)] = meta
        masks = pair_masks(meta.reshape(2 * ROWS, META).astype(F32))
        selector = jnp.transpose((masks[0] | masks[1]).astype(F32)).astype(BF16)

        @pl.loop(0, WIDTH_B // TILE)
        def _(tile):
            rows = zb[pl.ds(2 * pair, 2), :, tile_at(tile)].reshape(2 * ROWS, TILE)
            out = matmul(selector, rows).astype(BF16).reshape(EXPERTS, TWICE, TILE)
            xs[:, pair_at(pair), tile_at(tile)] = out

    xb_copies = []

    def send_pair(order):
        pair = pairs[order]
        select(pair)
        copies = []
        for step in range(1, EXPERTS):
            other = wrap(group + step)
            copy = remote(
                xs.at[other, pair_at(pair)], xr.at[group, pair_at(pair)],
                xb_send.at[order, step], xb_recv.at[order, step], {"group": other},
            )
            copies.append(start(copy))
        xb_copies.append(copies)
        xr[group, pair_at(pair)] = xs[group, pair_at(pair)]

    for hop in range(1, 4):
        ring_step(ring_b, hop)
        send_pair(hop - 1)
    for copy in xa_copies:
        copy.wait_recv()

    @pl.loop(0, HALF_A // TILE)
    def _(tile):
        rows = xa[:, :, tile_at(tile)].astype(F32)
        za[local, :, tile_at(tile)] = rows[:, :CAP].reshape(SLOTS, TILE).astype(BF16)
        za[local, :, tile_at(tile, HALF_A)] = rows[:, CAP:].reshape(SLOTS, TILE).astype(BF16)

    for piece in range(4):
        for way in range(2):
            start(ring_copy(ring_a, way, 1, piece))
    ring_step(ring_b, 4)
    send_pair(3)

    def add_a(block):
        block = wrap(block)
        rows = za[block]
        for half, weights in enumerate((wg_ref, wu_ref)):
            out = matmul(rows, weights[:WIDTH_A, :]).reshape(EXPERTS, CAP, HIDDEN)
            hacc[block, :, :, half * HIDDEN : (half + 1) * HIDDEN] = out

    def finish(pair):
        rows = xr[:, pair_at(pair), :].reshape(EXPERTS * TWICE, WIDTH_B)
        parts = []
        for half, weights in enumerate((wg_ref, wu_ref)):
            out = matmul(rows, weights[WIDTH_A:, :]).reshape(EXPERTS, 2, CAP, HIDDEN)
            done = [
                hacc[2 * pair + block, :, :, half * HIDDEN : (half + 1) * HIDDEN] + out[:, block]
                for block in range(2)
            ]
            parts.append(done)
        active = [jax.nn.silu(parts[0][block]) * parts[1][block] for block in range(2)]
        for block in range(2):
            acta_ref[2 * pair + block] = active[block].reshape(SLOTS, HIDDEN).astype(BF16)
        both = jnp.concatenate(active, axis=1)
        actb_ref[pair] = both.reshape(EXPERTS * TWICE, HIDDEN).astype(BF16)

    def blocks_of(hop):
        if hop == 0:
            return 1, lambda i: local
        if hop == 4:
            return 1, lambda i: local + 4
        return 2, lambda i: local - hop + 2 * hop * i

    def take(hop):
        count, place = blocks_of(hop)

        @pl.loop(0, count)
        def _(i):
            add_a(place(i))

    take(0)
    for hop in range(1, 5):
        ring_step(ring_a, hop)
        take(hop)
        for copy in xb_copies[hop - 1]:
            copy.wait_recv()
        finish(pairs[hop - 1])

    for copy in sent:
        copy.wait_send()


def combine_kernel(
    acta_ref, actb_ref, wd_ref, meta_ref, inc_ref, out_ref,
    za, ru, rd, hu, hd, xs, xr, tb, tu, td, sb, ra,
    xb_send, xb_recv, za_send, za_recv, zb_send, zb_recv, xa_send, xa_recv,
):
    group, local = lax.axis_index("group"), lax.axis_index("local")
    ring = ({"local": wrap(local + 1)}, {"local": wrap(local - 1)})
    sign = (1, -1)
    cuts_a, cuts_b = spans(WIDTH_A, PIECES), spans(WIDTH_B, 2)
    pairs = pairs_near_first(local)[::-1]
    sent = []

    barrier = pltpu.get_barrier_semaphore()
    for step in (1, 7):
        pl.semaphore_signal(barrier, inc=1, device_id={"local": wrap(local + step)})
    for step in range(1, EXPERTS):
        pl.semaphore_signal(barrier, inc=1, device_id={"group": wrap(group + step)})
    pl.semaphore_wait(barrier, 2 + EXPERTS - 1)

    def start(copy):
        copy.start()
        sent.append(copy)
        return copy

    def product_a(block):
        block = wrap(block)

        @pl.loop(0, WIDTH_A // TILE)
        def _(tile):
            za[block, :, tile_at(tile)] = matmul(acta_ref[block], wd_ref[:, tile_at(tile)]).astype(BF16)

    def product_both(distance):
        @pl.loop(0, 2)
        def _(i):
            product_a(local - distance + 2 * distance * i)

    def product_b(pair):
        @pl.loop(0, WIDTH_B // TILE)
        def _(tile):
            out = matmul(actb_ref[pair], wd_ref[:, tile_at(tile, WIDTH_A)]).astype(BF16)
            xs[:, pair_at(pair), tile_at(tile)] = out.reshape(EXPERTS, TWICE, TILE)

    def landing_a(way, hop, piece):
        begin, size = cuts_a[piece]
        if hop == 1:
            return (hu, hd)[way].at[:, pl.ds(begin - way * HALF_A, size)]
        return (ru, rd)[way].at[hop - 2, :, pl.ds(begin, size)]

    def landing_b(way, hop, piece):
        begin, size = cuts_b[piece]
        return (tu, td)[way].at[hop - 1, :, pl.ds(begin, size)]

    def ring_copy(kind, way, hop, piece):
        buffer, landing, sends, recvs, cuts = kind
        begin, size = cuts[piece]
        block = wrap(local + sign[way] * (5 - hop))
        return remote(
            buffer.at[block, :, pl.ds(begin, size)],
            landing(way, hop, piece),
            sends.at[way, hop - 1, piece],
            recvs.at[way, hop - 1, piece],
            ring[way],
        )

    def ring_open(kind, hop):
        for piece in range(len(kind[4])):
            for way in range(2):
                if hop == 5 - hops_of(piece, len(kind[4]), way):
                    start(ring_copy(kind, way, hop, piece))

    def ring_step(kind, hop):
        buffer, landing, _, _, cuts = kind
        for piece in range(len(cuts)):
            for way in range(2):
                if hop > 5 - hops_of(piece, len(cuts), way):
                    ring_copy(kind, way, hop - 1, piece).wait_recv()
                    begin, size = cuts[piece]
                    block = wrap(local + sign[way] * (5 - hop))
                    buffer[block, :, pl.ds(begin, size)] += landing(way, hop - 1, piece)[...]
                    start(ring_copy(kind, way, hop, piece))

    ring_a = (za, landing_a, za_send, za_recv, cuts_a)
    ring_b = (tb, landing_b, zb_send, zb_recv, cuts_b)
    xb_copies = []

    def send_pair(order):
        pair = pairs[order]
        product_b(pair)
        copies = []
        for step in range(1, EXPERTS):
            other = wrap(group + step)
            copy = remote(
                xs.at[other, pair_at(pair)], xr.at[group, pair_at(pair)],
                xb_send.at[order, step], xb_recv.at[order, step], {"group": other},
            )
            copies.append(start(copy))
        xb_copies.append(copies)
        xr[group, pair_at(pair)] = xs[group, pair_at(pair)]

    def mix_pair(order):
        pair = pairs[order]
        for copy in xb_copies[order]:
            copy.wait_recv()
        high, low = gate_matrices(meta_ref[pl.ds(2 * pair, 2)].reshape(2 * ROWS, META).astype(F32))

        @pl.loop(0, WIDTH_B // TILE)
        def _(tile):
            rows = xr[:, pair_at(pair), tile_at(tile)].reshape(EXPERTS * TWICE, TILE)
            mixed = matmul(high, rows) + matmul(low, rows)
            tb[pl.ds(2 * pair, 2), :, tile_at(tile)] = mixed.astype(BF16).reshape(2, ROWS, TILE)

    product_a(local + 4)
    ring_open(ring_a, 1)
    send_pair(0)
    product_both(3)
    ring_open(ring_a, 2)
    send_pair(1)
    ring_step(ring_a, 2)
    product_both(2)
    send_pair(2)
    ring_step(ring_a, 3)
    product_both(1)
    send_pair(3)
    product_a(local)
    mix_pair(0)
    ring_open(ring_b, 1)
    mix_pair(1)
    ring_open(ring_b, 2)
    ring_step(ring_b, 2)
    ring_step(ring_a, 4)
    mix_pair(2)
    for piece in range(PIECES):
        for way in range(2):
            ring_copy(ring_a, way, 4, piece).wait_recv()

    def total_a(columns):
        total = za[local, :, columns].astype(F32)
        total = total + ru[2, :, columns].astype(F32) + rd[2, :, columns].astype(F32)
        return total.reshape(EXPERTS, CAP, TILE)

    @pl.loop(0, HALF_A // TILE)
    def _(tile):
        halves = [total_a(tile_at(tile, base)) for base in (0, HALF_A)]
        sb[:, :, tile_at(tile)] = jnp.concatenate(halves, axis=1).astype(BF16)

    xa_copies = []
    for step in range(1, EXPERTS):
        other = wrap(group + step)
        copy = remote(
            sb.at[other], ra.at[group], xa_send.at[step], xa_recv.at[step], {"group": other}
        )
        xa_copies.append(start(copy))
    ra[group] = sb[group]
    ring_step(ring_b, 3)
    mix_pair(3)
    ring_step(ring_b, 4)

    own = meta_ref[local].astype(F32)
    high, low = gate_matrices(jnp.concatenate([own, own], axis=0))
    for copy in xa_copies:
        copy.wait_recv()

    @pl.loop(0, HALF_A // TILE)
    def _(tile):
        rows = ra[:, :, tile_at(tile)].reshape(EXPERTS * TWICE, TILE)
        mixed = matmul(high, rows) + matmul(low, rows)
        for half in range(2):
            columns = tile_at(tile, half * HALF_A)
            part = mixed[half * ROWS : (half + 1) * ROWS]
            out_ref[:, columns] = (inc_ref[:, columns].astype(F32) + part).astype(BF16)

    for piece in range(2):
        for way in range(2):
            ring_copy(ring_b, way, 4, piece).wait_recv()

    @pl.loop(0, WIDTH_B // TILE)
    def _(tile):
        columns, places = tile_at(tile), tile_at(tile, WIDTH_A)
        mixed = tb[local, :, columns].astype(F32)
        mixed = mixed + tu[3, :, columns].astype(F32) + td[3, :, columns].astype(F32)
        out_ref[:, places] = (inc_ref[:, places].astype(F32) + mixed).astype(BF16)

    for copy in sent:
        copy.wait_send()


def whole(*shape, dtype=BF16):
    return pltpu.VMEM(shape, dtype)


def dma(*shape):
    return pltpu.SemaphoreType.DMA(shape)


def params(number):
    return pltpu.CompilerParams(
        collective_id=number, has_side_effects=True, vmem_limit_bytes=VMEM_BYTES
    )


def per_device(hidden_in, norm_gain, router, w_gate, w_up, w_down, routes):
    vmem = pl.BlockSpec(memory_space=pltpu.VMEM)
    acta, actb, metas, incoming = pl.pallas_call(
        dispatch_kernel,
        out_shape=(
            jax.ShapeDtypeStruct((LOCALS, SLOTS, HIDDEN), BF16),
            jax.ShapeDtypeStruct((PAIRS, EXPERTS * TWICE, HIDDEN), BF16),
            jax.ShapeDtypeStruct((LOCALS, ROWS, META), BF16),
            jax.ShapeDtypeStruct((ROWS, WIDTH), BF16),
        ),
        in_specs=[vmem] * 6,
        out_specs=(vmem,) * 4,
        scratch_shapes=[
            whole(ROWS, WIDTH),
            whole(ROWS, WIDTH_A),
            whole(EXPERTS, TWICE, HALF_A),
            whole(EXPERTS, TWICE, HALF_A),
            whole(LOCALS, SLOTS, WIDTH_A),
            whole(LOCALS, ROWS, WIDTH_BX),
            whole(EXPERTS, SLOTS, WIDTH_B),
            whole(EXPERTS, SLOTS, WIDTH_B),
            whole(LOCALS, EXPERTS, CAP, 2 * HIDDEN, dtype=F32),
            dma(CHUNKS), dma(CHUNKS), dma(8), dma(8), dma(2, 4, 4), dma(2, 4, 4),
            dma(2, 4, 4), dma(2, 4, 4), dma(4, 8), dma(4, 8),
        ],
        compiler_params=params(0),
        name="dispatch",
    )(hidden_in[0], norm_gain, router[0], routes[0], w_gate[0, 0], w_up[0, 0])

    mixed = pl.pallas_call(
        combine_kernel,
        out_shape=jax.ShapeDtypeStruct((ROWS, WIDTH), BF16),
        in_specs=[vmem] * 5,
        out_specs=vmem,
        scratch_shapes=[
            whole(LOCALS, SLOTS, WIDTH_A),
            whole(3, SLOTS, WIDTH_A),
            whole(3, SLOTS, WIDTH_A),
            whole(SLOTS, HALF_A),
            whole(SLOTS, HALF_A),
            whole(EXPERTS, SLOTS, WIDTH_B),
            whole(EXPERTS, SLOTS, WIDTH_B),
            whole(LOCALS, ROWS, WIDTH_B),
            whole(4, ROWS, WIDTH_B),
            whole(4, ROWS, WIDTH_B),
            whole(EXPERTS, TWICE, HALF_A),
            whole(EXPERTS, TWICE, HALF_A),
            dma(4, 8), dma(4, 8), dma(2, 4, 4), dma(2, 4, 4), dma(2, 4, 2), dma(2, 4, 2),
            dma(8), dma(8),
        ],
        compiler_params=params(1),
        name="combine",
    )(acta, actb, w_down[0, 0], metas, incoming)
    return mixed[None]


def solution(mesh):
    placed = (
        P("section", ("group", "local"), None),
        P("section", None),
        P("section", None, None),
        P("section", "group", None, "local"),
        P("section", "group", None, "local"),
        P("section", "group", "local", None),
        P("section", ("group", "local"), None),
    )
    return jax.shard_map(
        per_device,
        mesh=mesh,
        in_specs=placed,
        out_specs=P("section", ("group", "local"), None),
        check_vma=False,
    )
```

```python
import jax
import jax.numpy as jnp
from jax import lax
from jax.experimental import pallas as pl
from jax.experimental.pallas import tpu as pltpu
from jax.sharding import PartitionSpec as P

WIDTH = 7168
WIDTH_A = 3584
WIDTH_B = WIDTH - WIDTH_A
HALF = 1792
QUARTER = 896
META = 128
WIDTH_BX = META + WIDTH_B + META
GATES_AT = META + WIDTH_B
EXPERTS = 8
LOCALS = 8
SECTIONS = 4
ROWS = 64
CAP = 24
TWICE = 2 * CAP
SLOTS = EXPERTS * CAP
PAIRS = LOCALS // 2
HIDDEN = 256
TILE = 256
LANES = 128
VMEM_BYTES = 63 * 2**20

BF16 = jnp.bfloat16
F32 = jnp.float32


def wrap(value, count=8):
    return lax.rem(value + 2 * count, count)


def matmul(left, right):
    return jnp.dot(left, right, preferred_element_type=F32)


def lanes_at(start, size):
    return pl.ds(pl.multiple_of(start, LANES), size)


def pair_at(pair):
    return pl.ds(pl.multiple_of(pair * TWICE, TWICE), TWICE)


def remote(src, dst, send, recv, device):
    return pltpu.make_async_remote_copy(
        src_ref=src, dst_ref=dst, send_sem=send, recv_sem=recv, device_id=device
    )


def hops_of(piece, pieces, way):
    first = piece < pieces // 2
    return 4 if first == (way == 0) else 3


def pairs_near_first(local):
    own = local // 2
    odd = lax.rem(local, 2)
    return [own, wrap(own + 2 * odd - 1, PAIRS), wrap(own - 2 * odd + 1, PAIRS), wrap(own + 2, PAIRS)]


def slot_masks(meta, expert_of, slot_of):
    out = []
    for choice in range(2):
        expert = meta[:, 2 * choice : 2 * choice + 1]
        slot = meta[:, 2 * choice + 1 : 2 * choice + 2]
        out.append((expert_of == expert) & (slot_of == slot))
    return out


def pair_masks(meta):
    shape = (2 * ROWS, EXPERTS * TWICE)
    column = lax.broadcasted_iota(jnp.int32, shape, 1)
    inside = lax.rem(column, TWICE)
    owner = lax.broadcasted_iota(jnp.int32, shape, 0) // ROWS
    slot = jnp.where(inside // CAP == owner, lax.rem(inside, CAP), -1)
    return slot_masks(meta, (column // TWICE).astype(F32), slot.astype(F32))


def gate_matrices(meta, gates):
    masks = pair_masks(meta)
    out = []
    for part in range(2):
        first, second = gates[:, part : 1 + part], gates[:, 2 + part : 3 + part]
        out.append((jnp.where(masks[0], first, 0.0) + jnp.where(masks[1], second, 0.0)).astype(BF16))
    return out


def layer_kernel(
    hid_ref, gain_ref, router_ref, routes_ref, wg_hbm, wu_hbm, wd_hbm, out_ref,
    wg, wu, wd, inc, scale_out, scale_in, na, disp, xa, za, zd, zb, xs, xr, hacc, acta, actb, tu, td,
    w_sem, y_send, y_recv, xa_send, xa_recv, zb_send, zb_recv, za_send, za_recv, xb_send, xb_recv,
    free_x, free_z,
    xc_send, xc_recv, zc_send, zc_recv, ze_send, ze_recv, xe_send, xe_recv,
):
    section = lax.axis_index("section")
    group, local = lax.axis_index("group"), lax.axis_index("local")
    ring = ({"local": wrap(local + 1)}, {"local": wrap(local - 1)})
    after = {"section": wrap(section + 1, SECTIONS)}
    sign = (1, -1)
    pairs = pairs_near_first(local)

    barrier = pltpu.get_barrier_semaphore()
    pl.semaphore_signal(barrier, inc=1, device_id={"section": wrap(section - 1, SECTIONS)})
    for way in range(2):
        pl.semaphore_signal(barrier, inc=1, device_id=ring[way])
    for step in range(1, EXPERTS):
        pl.semaphore_signal(barrier, inc=1, device_id={"group": wrap(group + step)})
    loads = [
        pltpu.make_async_copy(hbm, here, w_sem.at[i])
        for i, (hbm, here) in enumerate(((wg_hbm, wg), (wu_hbm, wu), (wd_hbm, wd)))
    ]
    for load in loads:
        load.start()
    pl.semaphore_wait(barrier, 1 + 2 + EXPERTS - 1)

    def start(copy, into):
        copy.start()
        into.append(copy)
        return copy


    chunks = (WIDTH_A, 0, HALF, WIDTH_A + HALF)
    shifts = []
    for number, begin in enumerate(chunks):
        view = pl.ds(begin, HALF)
        shifts.append(
            remote(hid_ref.at[:, view], inc.at[:, view], y_send.at[number], y_recv.at[number], after)
        )
    shifts[0].start()
    squares = jnp.zeros((ROWS, 1), F32)
    for begin in chunks:
        values = hid_ref[:, pl.ds(begin, HALF)].astype(F32)
        squares = squares + jnp.sum(values * values, axis=-1, keepdims=True)
    scale_out[...] = jnp.broadcast_to(lax.rsqrt(squares / WIDTH + 1e-06), (ROWS, LANES))
    scale_copy = remote(scale_out, scale_in, y_send.at[4], y_recv.at[4], after)
    scale_copy.start()
    shifts[1].start()

    square = (ROWS, ROWS)
    down, across = lax.broadcasted_iota(jnp.int32, square, 0), lax.broadcasted_iota(jnp.int32, square, 1)
    lane = lax.broadcasted_iota(jnp.int32, (ROWS, META), 1)
    experts = []
    for choice in range(2):
        row = jnp.broadcast_to(routes_ref[choice : choice + 1, :].astype(F32), square)
        experts.append(jnp.sum(jnp.where(down == across, row, 0.0), axis=1, keepdims=True))
    named = [expert == lane.astype(F32) for expert in experts]
    counts = (named[0].astype(F32) + named[1].astype(F32)).astype(BF16)
    before = matmul((down > across).astype(F32).astype(BF16), counts)
    meta = jnp.zeros((ROWS, META), F32)
    for choice in range(2):
        slot = jnp.sum(jnp.where(named[choice], before, 0.0), axis=1, keepdims=True)
        meta = jnp.where(lane == 2 * choice, experts[choice], meta)
        meta = jnp.where(lane == 2 * choice + 1, slot, meta)

    column = lax.broadcasted_iota(jnp.int32, (ROWS, EXPERTS * 32), 1)
    masks = slot_masks(meta, (column // 32).astype(F32), lax.rem(column, 32).astype(F32))
    chosen = (masks[0] | masks[1]).astype(F32)
    chosen = jnp.transpose(jnp.concatenate([chosen, jnp.zeros_like(chosen)], axis=0))
    chosen = chosen.reshape(EXPERTS, 32, 2 * ROWS)[:, :CAP].reshape(SLOTS, 2 * ROWS)
    chosen = chosen[:, :ROWS].astype(BF16)

    def normed_chunk(number):
        shifts[number].wait_recv()
        if number + 2 < len(shifts):
            shifts[number].wait_send()
            shifts[number + 2].start()
        if number == 0:
            scale_copy.wait_recv()
        view = pl.ds(chunks[number], HALF)
        values = inc[:, view].astype(F32) * scale_in[:, :1]
        normed = (values * gain_ref[:, view].astype(F32)).astype(BF16)
        logits = lax.dot_general(
            normed, router_ref[:, view], (((1,), (1,)), ((), ())), preferred_element_type=F32
        )
        return normed, logits

    def view_a(block, piece):
        return za.at[block, :, pl.ds(piece * QUARTER, QUARTER)]

    def view_b(block, piece):
        return zb.at[block, :, pl.ds(piece * (WIDTH_BX // 2), WIDTH_BX // 2)]

    sent_a, sent_b = [], []
    ring_a = (view_a, 4, za_send, za_recv, sent_a)
    ring_b = (view_b, 2, zb_send, zb_recv, sent_b)

    def gather_copy(kind, way, hop, piece):
        view, _, sends, recvs, _ = kind
        there = view(wrap(local - sign[way] * (hop - 1)), piece)
        return remote(
            there, there, sends.at[way, hop - 1, piece], recvs.at[way, hop - 1, piece], ring[way]
        )

    def gather_open(kind, pieces):
        for piece in pieces:
            for way in range(2):
                start(gather_copy(kind, way, 1, piece), kind[4])

    def gather_step(kind, hop, pieces):
        for piece in pieces:
            for way in range(2):
                hops = hops_of(piece, kind[1], way)
                if hop <= hops:
                    gather_copy(kind, way, hop, piece).wait_recv()
                if hop < hops:
                    start(gather_copy(kind, way, hop + 1, piece), kind[4])

    xa_copies = ([], [])

    def spread(half, normed):
        na[...] = normed

        @pl.loop(0, QUARTER // LANES)
        def _(tile):
            parts = [
                matmul(chosen, na[:, lanes_at(base + tile * LANES, LANES)]).reshape(EXPERTS, CAP, LANES)
                for base in (0, QUARTER)
            ]
            disp[half, :, :, lanes_at(tile * LANES, LANES)] = jnp.concatenate(parts, axis=1).astype(BF16)

        for step in range(1, EXPERTS):
            other = wrap(group + step)
            copy = remote(
                disp.at[half, other], xa.at[half, group],
                xa_send.at[half, step], xa_recv.at[half, step], {"group": other},
            )
            start(copy, xa_copies[half])
        xa[half, group] = disp[half, group]

    def compact(half):
        for copy in xa_copies[half]:
            copy.wait_recv()

        @pl.loop(0, QUARTER // LANES)
        def _(tile):
            rows = xa[half, :, :, lanes_at(tile * LANES, LANES)].astype(F32)
            for quarter in range(2):
                part = rows[:, quarter * CAP : (quarter + 1) * CAP].reshape(SLOTS, LANES).astype(BF16)
                begin = half * HALF + quarter * QUARTER
                za[local, :, lanes_at(begin + tile * LANES, LANES)] = part

        gather_open(ring_a, (2 * half, 2 * half + 1))

    def select(pair, place):
        both = zb[pl.ds(2 * pair, 2), :, :META].reshape(2 * ROWS, META).astype(F32)
        masks = pair_masks(both)
        selector = jnp.transpose((masks[0] | masks[1]).astype(F32)).astype(BF16)

        @pl.loop(0, WIDTH_B // TILE)
        def _(tile):
            rows = zb[pl.ds(2 * pair, 2), :, lanes_at(META + tile * TILE, TILE)].reshape(2 * ROWS, TILE)
            out = matmul(selector, rows).astype(BF16).reshape(EXPERTS, TWICE, TILE)
            xs[place, :, :, lanes_at(tile * TILE, TILE)] = out

    def send_pair(pair, place, sends, recvs):
        copies = []
        for step in range(1, EXPERTS):
            other = wrap(group + step)
            copy = remote(
                xs.at[place, other], xr.at[group, pair_at(pair)], sends.at[step], recvs.at[step],
                {"group": other},
            )
            start(copy, copies)
        xr[group, pair_at(pair)] = xs[place, group]
        return copies

    xb_copies = []

    def give_pair(order):
        if order >= 2:
            for copy in xb_copies[order - 2]:
                copy.wait_send()
        select(pairs[order], order % 2)
        xb_copies.append(send_pair(pairs[order], order % 2, xb_send.at[order], xb_recv.at[order]))

    normed, logits = normed_chunk(0)
    zb[local, :, :META] = meta.astype(BF16)
    zb[local, :, META : META + HALF] = normed
    gather_open(ring_b, (0,))
    normed, more = normed_chunk(1)
    logits = logits + more
    spread(0, normed)
    gather_step(ring_b, 1, (0,))
    normed, more = normed_chunk(2)
    logits = logits + more
    spread(1, normed)
    gather_step(ring_b, 2, (0,))
    normed, more = normed_chunk(3)
    zb[local, :, META + HALF : GATES_AT] = normed
    affinity = jax.nn.sigmoid(logits + more)
    expert = lax.broadcasted_iota(jnp.int32, (ROWS, EXPERTS), 1).astype(F32)
    picked = [
        jnp.sum(jnp.where(experts[choice] == expert, affinity, 0.0), axis=1, keepdims=True)
        for choice in range(2)
    ]
    gates = jnp.zeros((ROWS, META), F32)
    for choice in range(2):
        gate = 2.5 * picked[choice] / (picked[0] + picked[1])
        high = gate.astype(BF16).astype(F32)
        gates = jnp.where(lane == 2 * choice, high, gates)
        gates = jnp.where(lane == 2 * choice + 1, gate - high, gates)
    zb[local, :, GATES_AT:] = gates.astype(BF16)
    gather_open(ring_b, (1,))
    gather_step(ring_b, 3, (0,))
    compact(0)
    gather_step(ring_b, 1, (1,))
    give_pair(0)
    gather_step(ring_b, 4, (0,))
    compact(1)
    gather_step(ring_b, 2, (1,))
    give_pair(1)
    gather_step(ring_b, 3, (1,))
    gather_step(ring_b, 4, (1,))

    def add_a(block):
        block = wrap(block)
        rows = za[block]
        for half, weights in enumerate((wg, wu)):
            out = matmul(rows, weights[:WIDTH_A, :]).reshape(EXPERTS, CAP, HIDDEN)
            hacc[block, :, :, half * HIDDEN : (half + 1) * HIDDEN] = out

    def take(hop):
        count = 1 if hop in (0, 4) else 2

        @pl.loop(0, count)
        def _(i):
            add_a(local - hop + 2 * hop * i)

    def finish(order):
        pair = pairs[order]
        rows = xr[:, pair_at(pair), :].reshape(EXPERTS * TWICE, WIDTH_B)
        parts = []
        for half, weights in enumerate((wg, wu)):
            out = matmul(rows, weights[WIDTH_A:, :]).reshape(EXPERTS, 2, CAP, HIDDEN)
            done = [
                hacc[2 * pair + block, :, :, half * HIDDEN : (half + 1) * HIDDEN] + out[:, block]
                for block in range(2)
            ]
            parts.append(done)
        active = [jax.nn.silu(parts[0][block]) * parts[1][block] for block in range(2)]
        for block in range(2):
            acta[2 * pair + block] = active[block].reshape(SLOTS, HIDDEN).astype(BF16)
        both = jnp.concatenate(active, axis=1)
        actb[pair] = both.reshape(EXPERTS * TWICE, HIDDEN).astype(BF16)
        for step in range(1, EXPERTS):
            pl.semaphore_signal(free_x.at[order], inc=1, device_id={"group": wrap(group + step)})

    def product_b(pair, place):
        @pl.loop(0, WIDTH_B // TILE)
        def _(tile):
            weights = wd[:, lanes_at(WIDTH_A + tile * TILE, TILE)]
            out = matmul(actb[pair], weights).astype(BF16).reshape(EXPERTS, TWICE, TILE)
            xs[place, :, :, lanes_at(tile * TILE, TILE)] = out

    xc_copies = {}

    def return_pair(order, place, blocking):
        for copy in blocking:
            copy.wait_send()
        product_b(pairs[order], place)
        pl.semaphore_wait(free_x.at[order], EXPERTS - 1)
        xc_copies[order] = send_pair(pairs[order], place, xc_send.at[order], xc_recv.at[order])

    loads[0].wait()
    loads[1].wait()
    take(0)
    for hop in range(1, 5):
        gather_step(ring_a, hop, range(4))
        take(hop)
        if hop == 4:
            loads[2].wait()
            for copy in sent_a:
                copy.wait_send()
            for way in range(2):
                pl.semaphore_signal(free_z, inc=1, device_id=ring[way])
        for copy in xb_copies[hop - 1]:
            copy.wait_recv()
        if hop == 4:
            return_pair(0, 0, xb_copies[2])
        finish(hop - 1)
        if hop < 3:
            give_pair(hop + 1)


    sent_c = []

    def product_a(block, piece, fresh):
        block = wrap(block)

        def part(begin, size):
            columns = lanes_at(begin, size)
            out = matmul(acta[block], wd[:, columns])
            if not fresh:
                out = out + za[block, :, columns].astype(F32)
            za[block, :, columns] = out.astype(BF16)

        @pl.loop(0, QUARTER // TILE)
        def _(tile):
            part(piece * QUARTER + tile * TILE, TILE)

        part(piece * QUARTER + QUARTER // TILE * TILE, QUARTER % TILE)

    def sum_copy_a(way, hop, piece):
        block = wrap(local + sign[way] * (5 - hop))
        columns = pl.ds(piece * QUARTER, QUARTER)
        lands = zd.at[:, columns] if (way, hop) == (1, 4) else za.at[block, :, columns]
        return remote(
            za.at[block, :, columns], lands,
            zc_send.at[way, hop - 1, piece], zc_recv.at[way, hop - 1, piece], ring[way],
        )

    def sum_open_a(hop):
        for piece in range(4):
            for way in range(2):
                if hop == 5 - hops_of(piece, 4, way):
                    product_a(local + sign[way] * (5 - hop), piece, True)
                    start(sum_copy_a(way, hop, piece), sent_c)

    def sum_step_a(hop):
        for piece in range(4):
            for way in range(2):
                if hop > 5 - hops_of(piece, 4, way):
                    sum_copy_a(way, hop - 1, piece).wait_recv()
                    product_a(local + sign[way] * (5 - hop), piece, False)
                    start(sum_copy_a(way, hop, piece), sent_c)

    def sum_copy_b(way, hop, piece):
        block = wrap(local + sign[way] * (5 - hop))
        return remote(
            zb.at[block, :, pl.ds(META + piece * HALF, HALF)],
            (tu, td)[way].at[hop - 1, :, pl.ds(piece * HALF, HALF)],
            ze_send.at[way, hop - 1, piece], ze_recv.at[way, hop - 1, piece], ring[way],
        )

    def sum_step_b(hop):
        for piece in range(2):
            for way in range(2):
                opens = 5 - hops_of(piece, 2, way)
                if hop > opens:
                    sum_copy_b(way, hop - 1, piece).wait_recv()
                    block = wrap(local + sign[way] * (5 - hop))
                    came = (tu, td)[way][hop - 2, :, pl.ds(piece * HALF, HALF)]
                    zb[block, :, pl.ds(META + piece * HALF, HALF)] += came
                if hop >= opens:
                    start(sum_copy_b(way, hop, piece), sent_c)

    def mix_pair(order):
        pair = pairs[order]
        for copy in xc_copies[order]:
            copy.wait_recv()
        both = zb[pl.ds(2 * pair, 2), :, :META].reshape(2 * ROWS, META).astype(F32)
        weights = zb[pl.ds(2 * pair, 2), :, GATES_AT:].reshape(2 * ROWS, META).astype(F32)
        high, low = gate_matrices(both, weights)

        @pl.loop(0, WIDTH_B // TILE)
        def _(tile):
            rows = xr[:, pair_at(pair), lanes_at(tile * TILE, TILE)].reshape(EXPERTS * TWICE, TILE)
            mixed = matmul(high, rows) + matmul(low, rows)
            mixed = mixed.astype(BF16).reshape(2, ROWS, TILE)
            zb[pl.ds(2 * pair, 2), :, lanes_at(META + tile * TILE, TILE)] = mixed

    pl.semaphore_wait(free_z, 2)
    sum_open_a(1)
    return_pair(3, 1, xb_copies[3])
    sum_open_a(2)
    for copy in sent_b + xa_copies[0] + xa_copies[1]:
        copy.wait_send()
    sum_step_a(2)
    return_pair(2, 0, xc_copies[0])
    sum_step_a(3)
    return_pair(1, 1, xc_copies[3])
    mix_pair(3)
    sum_step_b(1)
    sum_step_a(4)
    mix_pair(2)
    sum_step_b(2)
    mix_pair(0)

    xe_copies = ([], [])

    def total_a(columns):
        total = matmul(acta[local], wd[:, columns])
        total = total + za[local, :, columns].astype(F32) + zd[:, columns].astype(F32)
        return total.reshape(EXPERTS, CAP, LANES)

    for half in range(2):
        for piece in (2 * half, 2 * half + 1):
            for way in range(2):
                sum_copy_a(way, 4, piece).wait_recv()

        @pl.loop(0, QUARTER // LANES)
        def _(tile, half=half):
            parts = [
                total_a(lanes_at(half * HALF + quarter * QUARTER + tile * LANES, LANES))
                for quarter in range(2)
            ]
            disp[half, :, :, lanes_at(tile * LANES, LANES)] = jnp.concatenate(parts, axis=1).astype(BF16)

        for step in range(1, EXPERTS):
            other = wrap(group + step)
            copy = remote(
                disp.at[half, other], xa.at[half, group],
                xe_send.at[half, step], xe_recv.at[half, step], {"group": other},
            )
            start(copy, xe_copies[half])
        xa[half, group] = disp[half, group]
    mix_pair(1)
    sum_step_b(3)
    sum_step_b(4)

    own, weights = zb[local, :, :META].astype(F32), zb[local, :, GATES_AT:].astype(F32)
    high, low = gate_matrices(
        jnp.concatenate([own, own], axis=0), jnp.concatenate([weights, weights], axis=0)
    )
    for half in range(2):
        for copy in xe_copies[half]:
            copy.wait_recv()

        @pl.loop(0, QUARTER // LANES)
        def _(tile, half=half):
            rows = xa[half, :, :, lanes_at(tile * LANES, LANES)].reshape(EXPERTS * TWICE, LANES)
            mixed = matmul(high, rows) + matmul(low, rows)
            for quarter in range(2):
                columns = lanes_at(half * HALF + quarter * QUARTER + tile * LANES, LANES)
                part = mixed[quarter * ROWS : (quarter + 1) * ROWS]
                out_ref[:, columns] = (inc[:, columns].astype(F32) + part).astype(BF16)

    for piece in range(2):
        for way in range(2):
            sum_copy_b(way, 4, piece).wait_recv()

    @pl.loop(0, WIDTH_B // TILE)
    def _(tile):
        columns = lanes_at(tile * TILE, TILE)
        places = lanes_at(WIDTH_A + tile * TILE, TILE)
        mixed = zb[local, :, lanes_at(META + tile * TILE, TILE)].astype(F32)
        mixed = mixed + tu[3, :, columns].astype(F32) + td[3, :, columns].astype(F32)
        out_ref[:, places] = (inc[:, places].astype(F32) + mixed).astype(BF16)

    scale_copy.wait_send()
    for copy in shifts[2:] + sent_c + xe_copies[0] + xe_copies[1] + xc_copies[2] + xc_copies[1]:
        copy.wait_send()


def whole(*shape, dtype=BF16):
    return pltpu.VMEM(shape, dtype)


def dma(*shape):
    return pltpu.SemaphoreType.DMA(shape)


def per_device(hidden_in, norm_gain, router, w_gate, w_up, w_down, routes):
    vmem = pl.BlockSpec(memory_space=pltpu.VMEM)
    anywhere = pl.BlockSpec(memory_space=pl.ANY)
    out = pl.pallas_call(
        layer_kernel,
        out_shape=jax.ShapeDtypeStruct((ROWS, WIDTH), BF16),
        in_specs=[vmem] * 4 + [anywhere] * 3,
        out_specs=vmem,
        scratch_shapes=[
            whole(WIDTH, HIDDEN),
            whole(WIDTH, HIDDEN),
            whole(HIDDEN, WIDTH),
            whole(ROWS, WIDTH),
            whole(ROWS, LANES, dtype=F32),
            whole(ROWS, LANES, dtype=F32),
            whole(ROWS, HALF),
            whole(2, EXPERTS, TWICE, QUARTER),
            whole(2, EXPERTS, TWICE, QUARTER),
            whole(LOCALS, SLOTS, WIDTH_A),
            whole(SLOTS, WIDTH_A),
            whole(LOCALS, ROWS, WIDTH_BX),
            whole(2, EXPERTS, TWICE, WIDTH_B),
            whole(EXPERTS, SLOTS, WIDTH_B),
            whole(LOCALS, EXPERTS, CAP, 2 * HIDDEN, dtype=F32),
            whole(LOCALS, SLOTS, HIDDEN),
            whole(PAIRS, EXPERTS * TWICE, HIDDEN),
            whole(4, ROWS, WIDTH_B),
            whole(4, ROWS, WIDTH_B),
            dma(3), dma(5), dma(5), dma(2, 8), dma(2, 8), dma(2, 4, 2), dma(2, 4, 2),
            dma(2, 4, 4), dma(2, 4, 4), dma(4, 8), dma(4, 8),
            pltpu.SemaphoreType.REGULAR((4,)), pltpu.SemaphoreType.REGULAR,
            dma(4, 8), dma(4, 8), dma(2, 4, 4), dma(2, 4, 4), dma(2, 4, 2), dma(2, 4, 2),
            dma(2, 8), dma(2, 8),
        ],
        compiler_params=pltpu.CompilerParams(
            collective_id=0, has_side_effects=True, vmem_limit_bytes=VMEM_BYTES
        ),
        name="layer",
    )(hidden_in[0], norm_gain, router[0].T, routes[0].T, w_gate[0, 0], w_up[0, 0], w_down[0, 0])
    return out[None]


def solution(mesh):
    placed = (
        P("section", ("group", "local"), None),
        P("section", None),
        P("section", None, None),
        P("section", "group", None, "local"),
        P("section", "group", None, "local"),
        P("section", "group", "local", None),
        P("section", ("group", "local"), None),
    )
    return jax.shard_map(
        per_device,
        mesh=mesh,
        in_specs=placed,
        out_specs=P("section", ("group", "local"), None),
        check_vma=False,
    )
```

```python
import jax
import jax.numpy as jnp
from jax import lax
from jax.experimental import pallas as pl
from jax.experimental.pallas import tpu as pltpu
from jax.sharding import PartitionSpec as P

WIDTH = 7168
WIDTH_A = 3584
WIDTH_B = WIDTH - WIDTH_A
META = 128
QUARTER = 896
QUARTERS = ((0, 896), (896, 896), (1792, 896), (2688, 896))
PARTS = ((0, 1792), (1792, WIDTH_B - 1792))
WIDTH_BX = META + WIDTH_B
EXPERTS = 8
LOCALS = 8
SECTIONS = 4
ROWS = 64
CAP = 24
TWICE = 2 * CAP
SLOTS = EXPERTS * CAP
PAIRS = LOCALS // 2
HIDDEN = 256
TILE = 256
LANES = 128
VMEM_BYTES = 63 * 2**20

BF16 = jnp.bfloat16
F32 = jnp.float32


def wrap(value, count=8):
    return lax.rem(value + 2 * count, count)


def matmul(left, right):
    return jnp.dot(left, right, preferred_element_type=F32)


def lanes_at(start, size):
    return pl.ds(pl.multiple_of(start, LANES), size)


def sweep(width, part):
    @pl.loop(0, width // TILE)
    def _(tile):
        part(tile * TILE, TILE)

    if width % TILE:
        part(width // TILE * TILE, width % TILE)


def pair_at(pair):
    return pl.ds(pl.multiple_of(pair * TWICE, TWICE), TWICE)


def remote(src, dst, send, recv, device):
    return pltpu.make_async_remote_copy(
        src_ref=src, dst_ref=dst, send_sem=send, recv_sem=recv, device_id=device
    )


def peers_of(group):
    chip, core = group // 2, lax.rem(group, 2)
    out = []
    for index, (ahead, flip) in enumerate(((1, 0), (3, 0), (2, 0), (1, 1), (3, 1), (2, 1), (0, 1))):
        there = 1 - core if flip else core
        out.append((index, wrap(chip + ahead, 4) * 2 + there))
    return out


def hops_of(piece, pieces, way):
    first = piece < pieces // 2
    return 4 if first == (way == 0) else 3


def pairs_near_first(local):
    own = local // 2
    odd = lax.rem(local, 2)
    return [own, wrap(own + 2 * odd - 1, PAIRS), wrap(own - 2 * odd + 1, PAIRS), wrap(own + 2, PAIRS)]


def slot_masks(meta, expert_of, slot_of):
    out = []
    for choice in range(2):
        expert = meta[:, 2 * choice : 2 * choice + 1]
        slot = meta[:, 2 * choice + 1 : 2 * choice + 2]
        out.append((expert_of == expert) & (slot_of == slot))
    return out


def pair_masks(meta):
    shape = (2 * ROWS, EXPERTS * TWICE)
    column = lax.broadcasted_iota(jnp.int32, shape, 1)
    inside = lax.rem(column, TWICE)
    owner = lax.broadcasted_iota(jnp.int32, shape, 0) // ROWS
    slot = jnp.where(inside // CAP == owner, lax.rem(inside, CAP), -1)
    return slot_masks(meta, (column // TWICE).astype(F32), slot.astype(F32))


def gate_matrices(meta, gates):
    masks = pair_masks(meta)
    out = []
    for part in range(2):
        first, second = gates[:, part : 1 + part], gates[:, 2 + part : 3 + part]
        out.append((jnp.where(masks[0], first, 0.0) + jnp.where(masks[1], second, 0.0)).astype(BF16))
    return out


def layer_kernel(
    hid_ref, gain_ref, router_ref, routes_ref, wg_hbm, wu_hbm, wd_hbm, out_ref,
    wg, wu, wd, inc, scale_out, scale_in, na, disp, xa, za, zd, zb, zg, xs, xr, hacc, acta, actb, tu, td,
    w_sem, y_send, y_recv, xa_send, xa_recv, zb_send, zb_recv, zg_send, zg_recv, za_send, za_recv,
    xb_send, xb_recv, free_x, free_z,
    xc_send, xc_recv, zc_send, zc_recv, ze_send, ze_recv, xe_send, xe_recv,
):
    section = lax.axis_index("section")
    group, local = lax.axis_index("group"), lax.axis_index("local")
    ring = ({"local": wrap(local + 1)}, {"local": wrap(local - 1)})
    after = {"section": wrap(section + 1, SECTIONS)}
    sign = (1, -1)
    pairs = pairs_near_first(local)
    peers = peers_of(group)

    barrier = pltpu.get_barrier_semaphore()
    pl.semaphore_signal(barrier, inc=1, device_id={"section": wrap(section - 1, SECTIONS)})
    for way in range(2):
        pl.semaphore_signal(barrier, inc=1, device_id=ring[way])
    for _, other in peers:
        pl.semaphore_signal(barrier, inc=1, device_id={"group": other})
    loads = [
        pltpu.make_async_copy(hbm, here, w_sem.at[i])
        for i, (hbm, here) in enumerate(((wg_hbm, wg), (wu_hbm, wu), (wd_hbm, wd)))
    ]
    for load in loads:
        load.start()

    def start(copy, into):
        copy.start()
        into.append(copy)
        return copy


    chunks = tuple((WIDTH_A + begin, size) for begin, size in PARTS)
    chunks += ((0, 2 * QUARTER), (2 * QUARTER, WIDTH_A - 2 * QUARTER))
    shifts = []
    for number, (begin, size) in enumerate(chunks):
        view = pl.ds(begin, size)
        shifts.append(
            remote(hid_ref.at[:, view], inc.at[:, view], y_send.at[number], y_recv.at[number], after)
        )
    squares = jnp.zeros((ROWS, 1), F32)
    for begin, size in chunks:
        values = hid_ref[:, pl.ds(begin, size)].astype(F32)
        squares = squares + jnp.sum(values * values, axis=-1, keepdims=True)
    scale_out[...] = jnp.broadcast_to(lax.rsqrt(squares / WIDTH + 1e-06), (ROWS, LANES))
    scale_copy = remote(scale_out, scale_in, y_send.at[4], y_recv.at[4], after)
    pl.semaphore_wait(barrier, 1 + 2 + EXPERTS - 1)
    scale_copy.start()
    shifts[0].start()
    shifts[1].start()

    square = (ROWS, ROWS)
    down, across = lax.broadcasted_iota(jnp.int32, square, 0), lax.broadcasted_iota(jnp.int32, square, 1)
    lane = lax.broadcasted_iota(jnp.int32, (ROWS, META), 1)
    experts = []
    for choice in range(2):
        row = jnp.broadcast_to(routes_ref[choice : choice + 1, :].astype(F32), square)
        experts.append(jnp.sum(jnp.where(down == across, row, 0.0), axis=1, keepdims=True))
    named = [expert == lane.astype(F32) for expert in experts]
    counts = (named[0].astype(F32) + named[1].astype(F32)).astype(BF16)
    before = matmul((down > across).astype(F32).astype(BF16), counts)
    meta = jnp.zeros((ROWS, META), F32)
    for choice in range(2):
        slot = jnp.sum(jnp.where(named[choice], before, 0.0), axis=1, keepdims=True)
        meta = jnp.where(lane == 2 * choice, experts[choice], meta)
        meta = jnp.where(lane == 2 * choice + 1, slot, meta)

    column = lax.broadcasted_iota(jnp.int32, (ROWS, EXPERTS * 32), 1)
    masks = slot_masks(meta, (column // 32).astype(F32), lax.rem(column, 32).astype(F32))
    chosen = (masks[0] | masks[1]).astype(F32)
    chosen = jnp.transpose(jnp.concatenate([chosen, jnp.zeros_like(chosen)], axis=0))
    chosen = chosen.reshape(EXPERTS, 32, 2 * ROWS)[:, :CAP].reshape(SLOTS, 2 * ROWS)
    chosen = chosen[:, :ROWS].astype(BF16)

    def normed_chunk(number):
        shifts[number].wait_recv()
        if number + 2 < len(shifts):
            shifts[number].wait_send()
            shifts[number + 2].start()
        if number == 0:
            scale_copy.wait_recv()
        view = pl.ds(*chunks[number])
        values = inc[:, view].astype(F32) * scale_in[:, :1]
        normed = (values * gain_ref[:, view].astype(F32)).astype(BF16)
        logits = lax.dot_general(
            normed, router_ref[:, view], (((1,), (1,)), ((), ())), preferred_element_type=F32
        )
        return normed, logits

    def view_a(block, piece):
        return za.at[block, :, pl.ds(*QUARTERS[piece])]

    def view_b(block, piece):
        begin, size = PARTS[piece]
        return zb.at[block, :, pl.ds(META + begin, size) if piece else pl.ds(0, META + size)]

    def view_g(block, piece):
        return zg.at[block]

    sent_a, sent_b = [], []
    ring_a = (view_a, 4, za_send, za_recv, sent_a)
    ring_b = (view_b, 2, zb_send, zb_recv, sent_b)
    ring_g = (view_g, 2, zg_send, zg_recv, sent_b)

    def gather_copy(kind, way, hop, piece):
        view, _, sends, recvs, _ = kind
        there = view(wrap(local - sign[way] * (hop - 1)), piece)
        return remote(
            there, there, sends.at[way, hop - 1, piece], recvs.at[way, hop - 1, piece], ring[way]
        )

    def gather_open(kind, pieces):
        for piece in pieces:
            for way in range(2):
                start(gather_copy(kind, way, 1, piece), kind[4])

    def gather_step(kind, hop, pieces):
        for piece in pieces:
            for way in range(2):
                hops = hops_of(piece, kind[1], way)
                if hop <= hops:
                    gather_copy(kind, way, hop, piece).wait_recv()
                if hop < hops:
                    start(gather_copy(kind, way, hop + 1, piece), kind[4])

    xa_copies = ([], [])

    def by_quarters(half, part):
        few = QUARTERS[2 * half + 1][1] // LANES

        @pl.loop(0, few)
        def _(tile):
            part(tile * LANES, 2)

        if few * LANES < QUARTER:
            part(few * LANES, 1)

    def stacked(parts):
        if len(parts) == 1:
            parts = parts + [jnp.zeros_like(parts[0])]
        return jnp.concatenate(parts, axis=1).astype(BF16)

    def exchange(half, sends, recvs, copies):
        for step, other in peers:
            copy = remote(
                disp.at[half, other], xa.at[half, group], sends.at[half, step], recvs.at[half, step],
                {"group": other},
            )
            start(copy, copies)
        xa[half, group] = disp[half, group]

    def spread(half, normed):
        na[:, : normed.shape[1]] = normed

        def part(begin, quarters):
            parts = [
                matmul(chosen, na[:, lanes_at(quarter * QUARTER + begin, LANES)])
                for quarter in range(quarters)
            ]
            parts = [rows.reshape(EXPERTS, CAP, LANES) for rows in parts]
            disp[half, :, :, lanes_at(begin, LANES)] = stacked(parts)

        by_quarters(half, part)
        exchange(half, xa_send, xa_recv, xa_copies[half])

    def compact(half):
        for copy in xa_copies[half]:
            copy.wait_recv()

        def part(begin, quarters):
            rows = xa[half, :, :, lanes_at(begin, LANES)].astype(F32)
            for quarter in range(quarters):
                some = rows[:, quarter * CAP : (quarter + 1) * CAP].reshape(SLOTS, LANES)
                columns = lanes_at((2 * half + quarter) * QUARTER + begin, LANES)
                za[local, :, columns] = some.astype(BF16)

        by_quarters(half, part)
        gather_open(ring_a, (2 * half, 2 * half + 1))

    def select(pair, place, begin, width):
        both = zb[pl.ds(2 * pair, 2), :, :META].reshape(2 * ROWS, META).astype(F32)
        masks = pair_masks(both)
        selector = jnp.transpose((masks[0] | masks[1]).astype(F32)).astype(BF16)

        def part(start, size):
            rows = zb[pl.ds(2 * pair, 2), :, lanes_at(META + begin + start, size)]
            out = matmul(selector, rows.reshape(2 * ROWS, size)).astype(BF16)
            xs[place, :, :, lanes_at(begin + start, size)] = out.reshape(EXPERTS, TWICE, size)

        sweep(width, part)

    def send_pair(pair, place, sends, recvs, begin=0, width=WIDTH_B):
        copies = []
        columns = pl.ds(begin, width)
        for step, other in peers:
            copy = remote(
                xs.at[place, other, :, columns], xr.at[group, pair_at(pair), columns],
                sends.at[step], recvs.at[step], {"group": other},
            )
            start(copy, copies)
        xr[group, pair_at(pair), columns] = xs[place, group, :, columns]
        return copies

    xb_copies = [[], [], [], []]

    def give_pair(order, begin=0, width=WIDTH_B):
        if order == 3:
            for copy in xb_copies[0]:
                copy.wait_send()
        select(pairs[order], order % 3, begin, width)
        row = order if begin == 0 else 4
        xb_copies[order] += send_pair(
            pairs[order], order % 3, xb_send.at[row], xb_recv.at[row], begin, width
        )

    normed, logits = normed_chunk(0)
    zb[local, :, :META] = meta.astype(BF16)
    zb[local, :, META : META + PARTS[1][0]] = normed
    gather_open(ring_b, (0,))
    normed, more = normed_chunk(1)
    logits = logits + more
    zb[local, :, META + PARTS[1][0] :] = normed
    gather_open(ring_b, (1,))
    gather_step(ring_b, 1, (0,))
    give_pair(0, *PARTS[0])
    normed, more = normed_chunk(2)
    logits = logits + more
    spread(0, normed)
    gather_step(ring_b, 1, (1,))
    give_pair(0, *PARTS[1])
    gather_step(ring_b, 2, (0,))
    normed, more = normed_chunk(3)
    spread(1, normed)
    affinity = jax.nn.sigmoid(logits + more)
    expert = lax.broadcasted_iota(jnp.int32, (ROWS, EXPERTS), 1).astype(F32)
    picked = [
        jnp.sum(jnp.where(experts[choice] == expert, affinity, 0.0), axis=1, keepdims=True)
        for choice in range(2)
    ]
    gates = jnp.zeros((ROWS, META), F32)
    for choice in range(2):
        gate = 2.5 * picked[choice] / (picked[0] + picked[1])
        high = gate.astype(BF16).astype(F32)
        gates = jnp.where(lane == 2 * choice, high, gates)
        gates = jnp.where(lane == 2 * choice + 1, gate - high, gates)
    zg[local] = gates.astype(BF16)
    gather_open(ring_g, (0,))
    gather_step(ring_b, 2, (1,))
    give_pair(1)
    gather_step(ring_b, 3, (0,))
    compact(0)
    gather_step(ring_b, 3, (1,))
    compact(1)
    give_pair(2)
    gather_step(ring_b, 4, (0,))
    gather_step(ring_b, 4, (1,))
    gather_step(ring_g, 1, (0,))

    def add_a(block):
        block = wrap(block)
        rows = za[block]
        for half, weights in enumerate((wg, wu)):
            out = matmul(rows, weights[:WIDTH_A, :]).reshape(EXPERTS, CAP, HIDDEN)
            hacc[block, :, :, half * HIDDEN : (half + 1) * HIDDEN] = out

    def take(hop):
        count = 1 if hop in (0, 4) else 2

        @pl.loop(0, count)
        def _(i):
            add_a(local - hop + 2 * hop * i)

    def finish(order):
        pair = pairs[order]
        rows = xr[:, pair_at(pair), :].reshape(EXPERTS * TWICE, WIDTH_B)
        parts = []
        for half, weights in enumerate((wg, wu)):
            out = matmul(rows, weights[WIDTH_A:, :]).reshape(EXPERTS, 2, CAP, HIDDEN)
            done = [
                hacc[2 * pair + block, :, :, half * HIDDEN : (half + 1) * HIDDEN] + out[:, block]
                for block in range(2)
            ]
            parts.append(done)
        active = [jax.nn.silu(parts[0][block]) * parts[1][block] for block in range(2)]
        for block in range(2):
            acta[2 * pair + block] = active[block].reshape(SLOTS, HIDDEN).astype(BF16)
        both = jnp.concatenate(active, axis=1)
        actb[pair] = both.reshape(EXPERTS * TWICE, HIDDEN).astype(BF16)
        for _, other in peers:
            pl.semaphore_signal(free_x.at[order], inc=1, device_id={"group": other})

    def product_b(pair, place):
        def part(begin, size):
            out = matmul(actb[pair], wd[:, lanes_at(WIDTH_A + begin, size)]).astype(BF16)
            xs[place, :, :, lanes_at(begin, size)] = out.reshape(EXPERTS, TWICE, size)

        sweep(WIDTH_B, part)

    xc_copies = {}

    def return_pair(order, place, blocking, parts=((0, WIDTH_B),)):
        for copy in blocking:
            copy.wait_send()
        product_b(pairs[order], place)
        pl.semaphore_wait(free_x.at[order], EXPERTS - 1)
        xc_copies[order] = []
        for number, (begin, width) in enumerate(parts):
            row = 4 if number else order
            copies = send_pair(
                pairs[order], place, xc_send.at[row], xc_recv.at[row], begin, width
            )
            xc_copies[order].append(copies)

    loads[0].wait()
    loads[1].wait()
    take(0)
    for hop in range(1, 5):
        gather_step(ring_a, hop, range(4))
        if hop < 4:
            gather_step(ring_g, hop + 1, (0,))
        take(hop)
        if hop == 4:
            loads[2].wait()
            for copy in sent_a:
                copy.wait_send()
            for way in range(2):
                pl.semaphore_signal(free_z, inc=1, device_id=ring[way])
        for copy in xb_copies[hop - 1]:
            copy.wait_recv()
        if hop == 4:
            return_pair(1, 1, xb_copies[1])
        finish(hop - 1)
        if hop == 1:
            give_pair(3)


    sent_c = []

    def product_a(block, piece, fresh):
        block = wrap(block)

        base, width = QUARTERS[piece]

        def part(begin, size):
            columns = lanes_at(base + begin, size)
            out = matmul(acta[block], wd[:, columns])
            if not fresh:
                out = out + za[block, :, columns].astype(F32)
            za[block, :, columns] = out.astype(BF16)

        sweep(width, part)

    def sum_copy_a(way, hop, piece):
        block = wrap(local + sign[way] * (5 - hop))
        columns = pl.ds(*QUARTERS[piece])
        lands = zd.at[:, columns] if (way, hop) == (1, 4) else za.at[block, :, columns]
        return remote(
            za.at[block, :, columns], lands,
            zc_send.at[way, hop - 1, piece], zc_recv.at[way, hop - 1, piece], ring[way],
        )

    def sum_open_a(hop):
        for piece in range(4):
            for way in range(2):
                if hop == 5 - hops_of(piece, 4, way):
                    product_a(local + sign[way] * (5 - hop), piece, True)
                    start(sum_copy_a(way, hop, piece), sent_c)

    def sum_step_a(hop):
        for piece in range(4):
            for way in range(2):
                if hop > 5 - hops_of(piece, 4, way):
                    sum_copy_a(way, hop - 1, piece).wait_recv()
                    product_a(local + sign[way] * (5 - hop), piece, False)
                    start(sum_copy_a(way, hop, piece), sent_c)

    def sum_copy_b(way, hop, piece):
        block = wrap(local + sign[way] * (5 - hop))
        begin, size = PARTS[piece]
        return remote(
            zb.at[block, :, pl.ds(META + begin, size)],
            (tu, td)[way].at[hop - 1, :, pl.ds(begin, size)],
            ze_send.at[way, hop - 1, piece], ze_recv.at[way, hop - 1, piece], ring[way],
        )

    def sum_step_b(hop, pieces=(0, 1)):
        for piece in pieces:
            for way in range(2):
                opens = 5 - hops_of(piece, 2, way)
                if hop > opens:
                    sum_copy_b(way, hop - 1, piece).wait_recv()
                    block = wrap(local + sign[way] * (5 - hop))
                    begin, size = PARTS[piece]
                    came = (tu, td)[way][hop - 2, :, pl.ds(begin, size)]
                    zb[block, :, pl.ds(META + begin, size)] += came
                if hop >= opens:
                    start(sum_copy_b(way, hop, piece), sent_c)

    def mix_pair(order, number=0, base=0, width=WIDTH_B):
        pair = pairs[order]
        for copy in xc_copies[order][number]:
            copy.wait_recv()
        both = zb[pl.ds(2 * pair, 2), :, :META].reshape(2 * ROWS, META).astype(F32)
        weights = zg[pl.ds(2 * pair, 2)].reshape(2 * ROWS, META).astype(F32)
        high, low = gate_matrices(both, weights)

        def part(begin, size):
            rows = xr[:, pair_at(pair), lanes_at(base + begin, size)].reshape(EXPERTS * TWICE, size)
            mixed = matmul(high, rows) + matmul(low, rows)
            mixed = mixed.astype(BF16).reshape(2, ROWS, size)
            zb[pl.ds(2 * pair, 2), :, lanes_at(META + base + begin, size)] = mixed

        sweep(width, part)

    pl.semaphore_wait(free_z, 2)
    sum_open_a(1)
    return_pair(3, 2, xb_copies[2])
    sum_open_a(2)
    for copy in sent_b + xa_copies[0] + xa_copies[1]:
        copy.wait_send()
    sum_step_a(2)
    return_pair(2, 0, xb_copies[3])
    sum_step_a(3)
    return_pair(0, 1, xc_copies[1][0], PARTS)
    mix_pair(3)
    sum_step_b(1)
    sum_step_a(4)
    mix_pair(2)
    sum_step_b(2)
    mix_pair(1)

    xe_copies = ([], [])

    def total_a(columns):
        total = matmul(acta[local], wd[:, columns])
        total = total + za[local, :, columns].astype(F32) + zd[:, columns].astype(F32)
        return total.reshape(EXPERTS, CAP, LANES)

    for half in range(2):
        for piece in (2 * half, 2 * half + 1):
            for way in range(2):
                sum_copy_a(way, 4, piece).wait_recv()

        def part(begin, quarters, half=half):
            parts = [
                total_a(lanes_at((2 * half + quarter) * QUARTER + begin, LANES))
                for quarter in range(quarters)
            ]
            disp[half, :, :, lanes_at(begin, LANES)] = stacked(parts)

        by_quarters(half, part)
        exchange(half, xe_send, xe_recv, xe_copies[half])
    sum_step_b(3)
    for piece in range(2):
        mix_pair(0, piece, *PARTS[piece])
        sum_step_b(4, (piece,))

    own, weights = zb[local, :, :META].astype(F32), zg[local].astype(F32)
    high, low = gate_matrices(
        jnp.concatenate([own, own], axis=0), jnp.concatenate([weights, weights], axis=0)
    )
    for half in range(2):
        for copy in xe_copies[half]:
            copy.wait_recv()

        def part(begin, quarters, half=half):
            rows = xa[half, :, :, lanes_at(begin, LANES)].reshape(EXPERTS * TWICE, LANES)
            mixed = matmul(high, rows) + matmul(low, rows)
            for quarter in range(quarters):
                columns = lanes_at((2 * half + quarter) * QUARTER + begin, LANES)
                some = mixed[quarter * ROWS : (quarter + 1) * ROWS]
                out_ref[:, columns] = (inc[:, columns].astype(F32) + some).astype(BF16)

        by_quarters(half, part)

    for piece in range(2):
        for way in range(2):
            sum_copy_b(way, 4, piece).wait_recv()

    def close(begin, size):
        columns, places = lanes_at(begin, size), lanes_at(WIDTH_A + begin, size)
        mixed = zb[local, :, lanes_at(META + begin, size)].astype(F32)
        mixed = mixed + tu[3, :, columns].astype(F32) + td[3, :, columns].astype(F32)
        out_ref[:, places] = (inc[:, places].astype(F32) + mixed).astype(BF16)

    sweep(WIDTH_B, close)
    scale_copy.wait_send()
    for copy in shifts[2:] + sent_c + xe_copies[0] + xe_copies[1]:
        copy.wait_send()
    for copies in xc_copies[3] + xc_copies[2] + xc_copies[0]:
        for copy in copies:
            copy.wait_send()


def whole(*shape, dtype=BF16):
    return pltpu.VMEM(shape, dtype)


def dma(*shape):
    return pltpu.SemaphoreType.DMA(shape)


def per_device(hidden_in, norm_gain, router, w_gate, w_up, w_down, routes):
    vmem = pl.BlockSpec(memory_space=pltpu.VMEM)
    anywhere = pl.BlockSpec(memory_space=pl.ANY)
    out = pl.pallas_call(
        layer_kernel,
        out_shape=jax.ShapeDtypeStruct((ROWS, WIDTH), BF16),
        in_specs=[vmem] * 4 + [anywhere] * 3,
        out_specs=vmem,
        scratch_shapes=[
            whole(WIDTH, HIDDEN),
            whole(WIDTH, HIDDEN),
            whole(HIDDEN, WIDTH),
            whole(ROWS, WIDTH),
            whole(ROWS, LANES, dtype=F32),
            whole(ROWS, LANES, dtype=F32),
            whole(ROWS, 2 * QUARTER),
            whole(2, EXPERTS, TWICE, QUARTER),
            whole(2, EXPERTS, TWICE, QUARTER),
            whole(LOCALS, SLOTS, WIDTH_A),
            whole(SLOTS, WIDTH_A),
            whole(LOCALS, ROWS, WIDTH_BX),
            whole(LOCALS, ROWS, META),
            whole(3, EXPERTS, TWICE, WIDTH_B),
            whole(EXPERTS, SLOTS, WIDTH_B),
            whole(LOCALS, EXPERTS, CAP, 2 * HIDDEN, dtype=F32),
            whole(LOCALS, SLOTS, HIDDEN),
            whole(PAIRS, EXPERTS * TWICE, HIDDEN),
            whole(4, ROWS, WIDTH_B),
            whole(4, ROWS, WIDTH_B),
            dma(3), dma(5), dma(5), dma(2, 8), dma(2, 8), dma(2, 4, 2), dma(2, 4, 2),
            dma(2, 4, 1), dma(2, 4, 1), dma(2, 4, 4), dma(2, 4, 4), dma(5, 8), dma(5, 8),
            pltpu.SemaphoreType.REGULAR((4,)), pltpu.SemaphoreType.REGULAR,
            dma(5, 8), dma(5, 8), dma(2, 4, 4), dma(2, 4, 4), dma(2, 4, 2), dma(2, 4, 2),
            dma(2, 8), dma(2, 8),
        ],
        compiler_params=pltpu.CompilerParams(
            collective_id=0, has_side_effects=True, vmem_limit_bytes=VMEM_BYTES
        ),
        name="layer",
    )(hidden_in[0], norm_gain, router[0].T, routes[0].T, w_gate[0, 0], w_up[0, 0], w_down[0, 0])
    return out[None]


def solution(mesh):
    placed = (
        P("section", ("group", "local"), None),
        P("section", None),
        P("section", None, None),
        P("section", "group", None, "local"),
        P("section", "group", None, "local"),
        P("section", "group", "local", None),
        P("section", ("group", "local"), None),
    )
    return jax.shard_map(
        per_device,
        mesh=mesh,
        in_specs=placed,
        out_specs=P("section", ("group", "local"), None),
        check_vma=False,
    )
```

```python
import jax
import jax.numpy as jnp
from jax import lax
from jax.experimental import pallas as pl
from jax.experimental.pallas import tpu as pltpu
from jax.sharding import PartitionSpec as P

WIDTH = 7168
WIDTH_A = 3456
WIDTH_B = WIDTH - WIDTH_A
META = 128
QUARTER = 896
QUARTERS = ((0, 896), (896, 896), (1792, 896), (2688, 768))
PARTS = ((0, 1792), (1792, WIDTH_B - 1792))
WIDTH_BX = META + WIDTH_B
EXPERTS = 8
LOCALS = 8
SECTIONS = 4
ROWS = 64
CAP = 24
TWICE = 2 * CAP
SLOTS = EXPERTS * CAP
PAIRS = LOCALS // 2
HIDDEN = 256
TILE = 256
LANES = 128
VMEM_BYTES = 63 * 2**20

BF16 = jnp.bfloat16
F32 = jnp.float32


def wrap(value, count=8):
    return lax.rem(value + 2 * count, count)


def matmul(left, right):
    return jnp.dot(left, right, preferred_element_type=F32)


def lanes_at(start, size):
    return pl.ds(pl.multiple_of(start, LANES), size)


def sweep(width, part):
    @pl.loop(0, width // TILE)
    def _(tile):
        part(tile * TILE, TILE)

    if width % TILE:
        part(width // TILE * TILE, width % TILE)


def pair_at(pair):
    return pl.ds(pl.multiple_of(pair * TWICE, TWICE), TWICE)


def remote(src, dst, send, recv, device):
    return pltpu.make_async_remote_copy(
        src_ref=src, dst_ref=dst, send_sem=send, recv_sem=recv, device_id=device
    )


def peers_of(group):
    chip, core = group // 2, lax.rem(group, 2)
    out = []
    for index, (ahead, flip) in enumerate(((1, 0), (3, 0), (2, 0), (1, 1), (3, 1), (2, 1), (0, 1))):
        there = 1 - core if flip else core
        out.append((index, wrap(chip + ahead, 4) * 2 + there))
    return out


def hops_of(piece, pieces, way):
    first = piece < pieces // 2
    return 4 if first == (way == 0) else 3


def pairs_near_first(local):
    own = local // 2
    odd = lax.rem(local, 2)
    return [own, wrap(own + 2 * odd - 1, PAIRS), wrap(own - 2 * odd + 1, PAIRS), wrap(own + 2, PAIRS)]


def slot_masks(meta, expert_of, slot_of):
    out = []
    for choice in range(2):
        expert = meta[:, 2 * choice : 2 * choice + 1]
        slot = meta[:, 2 * choice + 1 : 2 * choice + 2]
        out.append((expert_of == expert) & (slot_of == slot))
    return out


def pair_masks(meta):
    shape = (2 * ROWS, EXPERTS * TWICE)
    column = lax.broadcasted_iota(jnp.int32, shape, 1)
    inside = lax.rem(column, TWICE)
    owner = lax.broadcasted_iota(jnp.int32, shape, 0) // ROWS
    slot = jnp.where(inside // CAP == owner, lax.rem(inside, CAP), -1)
    return slot_masks(meta, (column // TWICE).astype(F32), slot.astype(F32))


def gate_matrices(meta, gates):
    masks = pair_masks(meta)
    out = []
    for part in range(2):
        first, second = gates[:, part : 1 + part], gates[:, 2 + part : 3 + part]
        out.append((jnp.where(masks[0], first, 0.0) + jnp.where(masks[1], second, 0.0)).astype(BF16))
    return out


def layer_kernel(
    hid_ref, gain_ref, router_ref, routes_ref, wg_hbm, wu_hbm, wd_hbm, out_ref,
    wg, wu, wd, inc, scale_out, scale_in, na, disp, xa, za, zd, zb, zg, xs, xr, hacc, acta, actb, tu, td,
    w_sem, y_send, y_recv, xa_send, xa_recv, zb_send, zb_recv, zg_send, zg_recv, za_send, za_recv,
    xb_send, xb_recv, free_x, free_z,
    xc_send, xc_recv, zc_send, zc_recv, ze_send, ze_recv, xe_send, xe_recv,
):
    section = lax.axis_index("section")
    group, local = lax.axis_index("group"), lax.axis_index("local")
    ring = ({"local": wrap(local + 1)}, {"local": wrap(local - 1)})
    after = {"section": wrap(section + 1, SECTIONS)}
    sign = (1, -1)
    pairs = pairs_near_first(local)
    peers = peers_of(group)

    barrier = pltpu.get_barrier_semaphore()
    pl.semaphore_signal(barrier, inc=1, device_id={"section": wrap(section - 1, SECTIONS)})
    for way in range(2):
        pl.semaphore_signal(barrier, inc=1, device_id=ring[way])
    for _, other in peers:
        pl.semaphore_signal(barrier, inc=1, device_id={"group": other})
    loads = [
        pltpu.make_async_copy(hbm, here, w_sem.at[i])
        for i, (hbm, here) in enumerate(((wg_hbm, wg), (wu_hbm, wu), (wd_hbm, wd)))
    ]
    for load in loads:
        load.start()

    def start(copy, into):
        copy.start()
        into.append(copy)
        return copy


    chunks = tuple((WIDTH_A + begin, size) for begin, size in PARTS)
    chunks += ((0, 2 * QUARTER), (2 * QUARTER, WIDTH_A - 2 * QUARTER))
    shifts = []
    for number, (begin, size) in enumerate(chunks):
        view = pl.ds(begin, size)
        shifts.append(
            remote(hid_ref.at[:, view], inc.at[:, view], y_send.at[number], y_recv.at[number], after)
        )
    squares = jnp.zeros((ROWS, 1), F32)
    for begin, size in chunks:
        values = hid_ref[:, pl.ds(begin, size)].astype(F32)
        squares = squares + jnp.sum(values * values, axis=-1, keepdims=True)
    scale_out[...] = jnp.broadcast_to(lax.rsqrt(squares / WIDTH + 1e-06), (ROWS, LANES))
    scale_copy = remote(scale_out, scale_in, y_send.at[4], y_recv.at[4], after)
    pl.semaphore_wait(barrier, 1 + 2 + EXPERTS - 1)
    scale_copy.start()
    shifts[0].start()
    shifts[1].start()

    square = (ROWS, ROWS)
    down, across = lax.broadcasted_iota(jnp.int32, square, 0), lax.broadcasted_iota(jnp.int32, square, 1)
    lane = lax.broadcasted_iota(jnp.int32, (ROWS, META), 1)
    experts = []
    for choice in range(2):
        row = jnp.broadcast_to(routes_ref[choice : choice + 1, :].astype(F32), square)
        experts.append(jnp.sum(jnp.where(down == across, row, 0.0), axis=1, keepdims=True))
    named = [expert == lane.astype(F32) for expert in experts]
    counts = (named[0].astype(F32) + named[1].astype(F32)).astype(BF16)
    before = matmul((down > across).astype(F32).astype(BF16), counts)
    meta = jnp.zeros((ROWS, META), F32)
    for choice in range(2):
        slot = jnp.sum(jnp.where(named[choice], before, 0.0), axis=1, keepdims=True)
        meta = jnp.where(lane == 2 * choice, experts[choice], meta)
        meta = jnp.where(lane == 2 * choice + 1, slot, meta)

    column = lax.broadcasted_iota(jnp.int32, (ROWS, EXPERTS * 32), 1)
    masks = slot_masks(meta, (column // 32).astype(F32), lax.rem(column, 32).astype(F32))
    chosen = (masks[0] | masks[1]).astype(F32)
    chosen = jnp.transpose(jnp.concatenate([chosen, jnp.zeros_like(chosen)], axis=0))
    chosen = chosen.reshape(EXPERTS, 32, 2 * ROWS)[:, :CAP].reshape(SLOTS, 2 * ROWS)
    chosen = chosen[:, :ROWS].astype(BF16)

    def normed_chunk(number):
        shifts[number].wait_recv()
        if number + 2 < len(shifts):
            shifts[number].wait_send()
            shifts[number + 2].start()
        if number == 0:
            scale_copy.wait_recv()
        view = pl.ds(*chunks[number])
        values = inc[:, view].astype(F32) * scale_in[:, :1]
        normed = (values * gain_ref[:, view].astype(F32)).astype(BF16)
        logits = lax.dot_general(
            normed, router_ref[:, view], (((1,), (1,)), ((), ())), preferred_element_type=F32
        )
        return normed, logits

    def view_a(block, piece):
        return za.at[block, :, pl.ds(*QUARTERS[piece])]

    def view_b(block, piece):
        begin, size = PARTS[piece]
        return zb.at[block, :, pl.ds(META + begin, size) if piece else pl.ds(0, META + size)]

    def view_g(block, piece):
        return zg.at[block]

    sent_a, sent_b = [], []
    ring_a = (view_a, 4, za_send, za_recv, sent_a)
    ring_b = (view_b, 2, zb_send, zb_recv, sent_b)
    ring_g = (view_g, 2, zg_send, zg_recv, sent_b)

    def gather_copy(kind, way, hop, piece):
        view, _, sends, recvs, _ = kind
        there = view(wrap(local - sign[way] * (hop - 1)), piece)
        return remote(
            there, there, sends.at[way, hop - 1, piece], recvs.at[way, hop - 1, piece], ring[way]
        )

    def gather_open(kind, pieces):
        for piece in pieces:
            for way in range(2):
                start(gather_copy(kind, way, 1, piece), kind[4])

    def gather_step(kind, hop, pieces):
        for piece in pieces:
            for way in range(2):
                hops = hops_of(piece, kind[1], way)
                if hop <= hops:
                    gather_copy(kind, way, hop, piece).wait_recv()
                if hop < hops:
                    start(gather_copy(kind, way, hop + 1, piece), kind[4])

    xa_copies = ([], [])

    def by_quarters(half, part):
        few = QUARTERS[2 * half + 1][1] // LANES

        @pl.loop(0, few)
        def _(tile):
            part(tile * LANES, 2)

        if few * LANES < QUARTER:
            part(few * LANES, 1)

    def stacked(parts):
        if len(parts) == 1:
            parts = parts + [jnp.zeros_like(parts[0])]
        return jnp.concatenate(parts, axis=1).astype(BF16)

    def exchange(half, sends, recvs, copies):
        for step, other in peers:
            copy = remote(
                disp.at[half, other], xa.at[half, group], sends.at[half, step], recvs.at[half, step],
                {"group": other},
            )
            start(copy, copies)
        xa[half, group] = disp[half, group]

    def spread(half, normed):
        na[:, : normed.shape[1]] = normed

        def part(begin, quarters):
            parts = [
                matmul(chosen, na[:, lanes_at(quarter * QUARTER + begin, LANES)])
                for quarter in range(quarters)
            ]
            parts = [rows.reshape(EXPERTS, CAP, LANES) for rows in parts]
            disp[half, :, :, lanes_at(begin, LANES)] = stacked(parts)

        by_quarters(half, part)
        exchange(half, xa_send, xa_recv, xa_copies[half])

    def compact(half):
        for copy in xa_copies[half]:
            copy.wait_recv()

        def part(begin, quarters):
            rows = xa[half, :, :, lanes_at(begin, LANES)].astype(F32)
            for quarter in range(quarters):
                some = rows[:, quarter * CAP : (quarter + 1) * CAP].reshape(SLOTS, LANES)
                columns = lanes_at((2 * half + quarter) * QUARTER + begin, LANES)
                za[local, :, columns] = some.astype(BF16)

        by_quarters(half, part)
        gather_open(ring_a, (2 * half, 2 * half + 1))

    def select(pair, place, begin, width):
        both = zb[pl.ds(2 * pair, 2), :, :META].reshape(2 * ROWS, META).astype(F32)
        masks = pair_masks(both)
        selector = jnp.transpose((masks[0] | masks[1]).astype(F32)).astype(BF16)

        def part(start, size):
            rows = zb[pl.ds(2 * pair, 2), :, lanes_at(META + begin + start, size)]
            out = matmul(selector, rows.reshape(2 * ROWS, size)).astype(BF16)
            xs[place, :, :, lanes_at(begin + start, size)] = out.reshape(EXPERTS, TWICE, size)

        sweep(width, part)

    def send_pair(pair, place, sends, recvs, begin=0, width=WIDTH_B):
        copies = []
        columns = pl.ds(begin, width)
        for step, other in peers:
            copy = remote(
                xs.at[place, other, :, columns], xr.at[group, pair_at(pair), columns],
                sends.at[step], recvs.at[step], {"group": other},
            )
            start(copy, copies)
        xr[group, pair_at(pair), columns] = xs[place, group, :, columns]
        return copies

    xb_copies = [[], [], [], []]

    def give_pair(order, begin=0, width=WIDTH_B):
        if order == 3:
            for copy in xb_copies[0]:
                copy.wait_send()
        select(pairs[order], order % 3, begin, width)
        row = order if begin == 0 else 4
        xb_copies[order] += send_pair(
            pairs[order], order % 3, xb_send.at[row], xb_recv.at[row], begin, width
        )

    normed, logits = normed_chunk(0)
    zb[local, :, :META] = meta.astype(BF16)
    zb[local, :, META : META + PARTS[1][0]] = normed
    gather_open(ring_b, (0,))
    normed, more = normed_chunk(1)
    logits = logits + more
    zb[local, :, META + PARTS[1][0] :] = normed
    gather_open(ring_b, (1,))
    gather_step(ring_b, 1, (0,))
    give_pair(0, *PARTS[0])
    normed, more = normed_chunk(2)
    logits = logits + more
    spread(0, normed)
    gather_step(ring_b, 1, (1,))
    give_pair(0, *PARTS[1])
    gather_step(ring_b, 2, (0,))
    normed, more = normed_chunk(3)
    spread(1, normed)
    affinity = jax.nn.sigmoid(logits + more)
    expert = lax.broadcasted_iota(jnp.int32, (ROWS, EXPERTS), 1).astype(F32)
    picked = [
        jnp.sum(jnp.where(experts[choice] == expert, affinity, 0.0), axis=1, keepdims=True)
        for choice in range(2)
    ]
    gates = jnp.zeros((ROWS, META), F32)
    for choice in range(2):
        gate = 2.5 * picked[choice] / (picked[0] + picked[1])
        high = gate.astype(BF16).astype(F32)
        gates = jnp.where(lane == 2 * choice, high, gates)
        gates = jnp.where(lane == 2 * choice + 1, gate - high, gates)
    zg[local] = gates.astype(BF16)
    gather_open(ring_g, (0,))
    gather_step(ring_b, 2, (1,))
    give_pair(1)
    gather_step(ring_b, 3, (0,))
    compact(0)
    gather_step(ring_b, 3, (1,))
    compact(1)
    give_pair(2)
    gather_step(ring_b, 4, (0,))
    gather_step(ring_b, 4, (1,))
    gather_step(ring_g, 1, (0,))

    def add_a(block):
        block = wrap(block)
        rows = za[block]
        for half, weights in enumerate((wg, wu)):
            out = matmul(rows, weights[:WIDTH_A, :]).reshape(EXPERTS, CAP, HIDDEN)
            hacc[block, :, :, half * HIDDEN : (half + 1) * HIDDEN] = out

    def take(hop):
        count = 1 if hop in (0, 4) else 2

        @pl.loop(0, count)
        def _(i):
            add_a(local - hop + 2 * hop * i)

    def finish(order):
        pair = pairs[order]
        rows = xr[:, pair_at(pair), :].reshape(EXPERTS * TWICE, WIDTH_B)
        parts = []
        for half, weights in enumerate((wg, wu)):
            out = matmul(rows, weights[WIDTH_A:, :]).reshape(EXPERTS, 2, CAP, HIDDEN)
            done = [
                hacc[2 * pair + block, :, :, half * HIDDEN : (half + 1) * HIDDEN] + out[:, block]
                for block in range(2)
            ]
            parts.append(done)
        active = [jax.nn.silu(parts[0][block]) * parts[1][block] for block in range(2)]
        for block in range(2):
            acta[2 * pair + block] = active[block].reshape(SLOTS, HIDDEN).astype(BF16)
        both = jnp.concatenate(active, axis=1)
        actb[pair] = both.reshape(EXPERTS * TWICE, HIDDEN).astype(BF16)
        for _, other in peers:
            pl.semaphore_signal(free_x.at[order], inc=1, device_id={"group": other})

    def product_b(pair, place):
        def part(begin, size):
            out = matmul(actb[pair], wd[:, lanes_at(WIDTH_A + begin, size)]).astype(BF16)
            xs[place, :, :, lanes_at(begin, size)] = out.reshape(EXPERTS, TWICE, size)

        sweep(WIDTH_B, part)

    xc_copies = {}

    def return_pair(order, place, blocking, parts=((0, WIDTH_B),)):
        if blocking is not None:
            for copy in blocking:
                copy.wait_send()
            product_b(pairs[order], place)
        pl.semaphore_wait(free_x.at[order], EXPERTS - 1)
        xc_copies[order] = []
        for number, (begin, width) in enumerate(parts):
            row = 4 if number else order
            copies = send_pair(
                pairs[order], place, xc_send.at[row], xc_recv.at[row], begin, width
            )
            xc_copies[order].append(copies)

    loads[0].wait()
    loads[1].wait()
    take(0)
    for hop in range(1, 5):
        if hop == 4:
            loads[2].wait()
            for copy in xb_copies[1]:
                copy.wait_send()
            product_b(pairs[1], 1)
        gather_step(ring_a, hop, range(4))
        if hop < 4:
            gather_step(ring_g, hop + 1, (0,))
        take(hop)
        if hop == 4:
            for copy in sent_a:
                copy.wait_send()
            for way in range(2):
                pl.semaphore_signal(free_z, inc=1, device_id=ring[way])
        for copy in xb_copies[hop - 1]:
            copy.wait_recv()
        if hop == 4:
            return_pair(1, 1, None)
        finish(hop - 1)
        if hop == 1:
            give_pair(3)


    sent_c = []

    def product_a(block, piece, fresh):
        block = wrap(block)

        base, width = QUARTERS[piece]

        def part(begin, size):
            columns = lanes_at(base + begin, size)
            out = matmul(acta[block], wd[:, columns])
            if not fresh:
                out = out + za[block, :, columns].astype(F32)
            za[block, :, columns] = out.astype(BF16)

        sweep(width, part)

    def sum_copy_a(way, hop, piece):
        block = wrap(local + sign[way] * (5 - hop))
        columns = pl.ds(*QUARTERS[piece])
        lands = zd.at[:, columns] if (way, hop) == (1, 4) else za.at[block, :, columns]
        return remote(
            za.at[block, :, columns], lands,
            zc_send.at[way, hop - 1, piece], zc_recv.at[way, hop - 1, piece], ring[way],
        )

    def sum_open_a(hop):
        for piece in range(4):
            for way in range(2):
                if hop == 5 - hops_of(piece, 4, way):
                    product_a(local + sign[way] * (5 - hop), piece, True)
                    start(sum_copy_a(way, hop, piece), sent_c)

    def sum_step_a(hop):
        for piece in range(4):
            for way in range(2):
                if hop > 5 - hops_of(piece, 4, way):
                    sum_copy_a(way, hop - 1, piece).wait_recv()
                    product_a(local + sign[way] * (5 - hop), piece, False)
                    start(sum_copy_a(way, hop, piece), sent_c)

    def sum_copy_b(way, hop, piece):
        block = wrap(local + sign[way] * (5 - hop))
        begin, size = PARTS[piece]
        return remote(
            zb.at[block, :, pl.ds(META + begin, size)],
            (tu, td)[way].at[hop - 1, :, pl.ds(begin, size)],
            ze_send.at[way, hop - 1, piece], ze_recv.at[way, hop - 1, piece], ring[way],
        )

    def sum_step_b(hop, pieces=(0, 1)):
        for piece in pieces:
            for way in range(2):
                opens = 5 - hops_of(piece, 2, way)
                if hop > opens:
                    sum_copy_b(way, hop - 1, piece).wait_recv()
                    block = wrap(local + sign[way] * (5 - hop))
                    begin, size = PARTS[piece]
                    came = (tu, td)[way][hop - 2, :, pl.ds(begin, size)]
                    zb[block, :, pl.ds(META + begin, size)] += came
                if hop >= opens:
                    start(sum_copy_b(way, hop, piece), sent_c)

    def mix_pair(order, number=0, base=0, width=WIDTH_B):
        pair = pairs[order]
        for copy in xc_copies[order][number]:
            copy.wait_recv()
        both = zb[pl.ds(2 * pair, 2), :, :META].reshape(2 * ROWS, META).astype(F32)
        weights = zg[pl.ds(2 * pair, 2)].reshape(2 * ROWS, META).astype(F32)
        high, low = gate_matrices(both, weights)

        def part(begin, size):
            rows = xr[:, pair_at(pair), lanes_at(base + begin, size)].reshape(EXPERTS * TWICE, size)
            mixed = matmul(high, rows) + matmul(low, rows)
            mixed = mixed.astype(BF16).reshape(2, ROWS, size)
            zb[pl.ds(2 * pair, 2), :, lanes_at(META + base + begin, size)] = mixed

        sweep(width, part)

    pl.semaphore_wait(free_z, 2)
    sum_open_a(1)
    return_pair(3, 2, xb_copies[2])
    sum_open_a(2)
    for copy in sent_b + xa_copies[0] + xa_copies[1]:
        copy.wait_send()
    sum_step_a(2)
    return_pair(2, 0, xb_copies[3])
    sum_step_a(3)
    return_pair(0, 1, xc_copies[1][0], PARTS)
    mix_pair(3)
    sum_step_b(1)
    sum_step_a(4)
    mix_pair(2)
    sum_step_b(2)
    mix_pair(1)

    xe_copies = ([], [])

    def total_a(columns):
        total = matmul(acta[local], wd[:, columns])
        total = total + za[local, :, columns].astype(F32) + zd[:, columns].astype(F32)
        return total.reshape(EXPERTS, CAP, LANES)

    for half in range(2):
        for piece in (2 * half, 2 * half + 1):
            for way in range(2):
                sum_copy_a(way, 4, piece).wait_recv()

        def part(begin, quarters, half=half):
            parts = [
                total_a(lanes_at((2 * half + quarter) * QUARTER + begin, LANES))
                for quarter in range(quarters)
            ]
            disp[half, :, :, lanes_at(begin, LANES)] = stacked(parts)

        by_quarters(half, part)
        exchange(half, xe_send, xe_recv, xe_copies[half])
    sum_step_b(3)
    for piece in range(2):
        mix_pair(0, piece, *PARTS[piece])
        sum_step_b(4, (piece,))

    own, weights = zb[local, :, :META].astype(F32), zg[local].astype(F32)
    high, low = gate_matrices(
        jnp.concatenate([own, own], axis=0), jnp.concatenate([weights, weights], axis=0)
    )
    for half in range(2):
        for copy in xe_copies[half]:
            copy.wait_recv()

        def part(begin, quarters, half=half):
            rows = xa[half, :, :, lanes_at(begin, LANES)].reshape(EXPERTS * TWICE, LANES)
            mixed = matmul(high, rows) + matmul(low, rows)
            for quarter in range(quarters):
                columns = lanes_at((2 * half + quarter) * QUARTER + begin, LANES)
                some = mixed[quarter * ROWS : (quarter + 1) * ROWS]
                out_ref[:, columns] = (inc[:, columns].astype(F32) + some).astype(BF16)

        by_quarters(half, part)

    for piece in range(2):
        for way in range(2):
            sum_copy_b(way, 4, piece).wait_recv()

    def close(begin, size):
        columns, places = lanes_at(begin, size), lanes_at(WIDTH_A + begin, size)
        mixed = zb[local, :, lanes_at(META + begin, size)].astype(F32)
        mixed = mixed + tu[3, :, columns].astype(F32) + td[3, :, columns].astype(F32)
        out_ref[:, places] = (inc[:, places].astype(F32) + mixed).astype(BF16)

    sweep(WIDTH_B, close)
    scale_copy.wait_send()
    for copy in shifts[2:] + sent_c + xe_copies[0] + xe_copies[1]:
        copy.wait_send()
    for copies in xc_copies[3] + xc_copies[2] + xc_copies[0]:
        for copy in copies:
            copy.wait_send()


def whole(*shape, dtype=BF16):
    return pltpu.VMEM(shape, dtype)


def dma(*shape):
    return pltpu.SemaphoreType.DMA(shape)


def per_device(hidden_in, norm_gain, router, w_gate, w_up, w_down, routes):
    vmem = pl.BlockSpec(memory_space=pltpu.VMEM)
    anywhere = pl.BlockSpec(memory_space=pl.ANY)
    out = pl.pallas_call(
        layer_kernel,
        out_shape=jax.ShapeDtypeStruct((ROWS, WIDTH), BF16),
        in_specs=[vmem] * 4 + [anywhere] * 3,
        out_specs=vmem,
        scratch_shapes=[
            whole(WIDTH, HIDDEN),
            whole(WIDTH, HIDDEN),
            whole(HIDDEN, WIDTH),
            whole(ROWS, WIDTH),
            whole(ROWS, LANES, dtype=F32),
            whole(ROWS, LANES, dtype=F32),
            whole(ROWS, 2 * QUARTER),
            whole(2, EXPERTS, TWICE, QUARTER),
            whole(2, EXPERTS, TWICE, QUARTER),
            whole(LOCALS, SLOTS, WIDTH_A),
            whole(SLOTS, WIDTH_A),
            whole(LOCALS, ROWS, WIDTH_BX),
            whole(LOCALS, ROWS, META),
            whole(3, EXPERTS, TWICE, WIDTH_B),
            whole(EXPERTS, SLOTS, WIDTH_B),
            whole(LOCALS, EXPERTS, CAP, 2 * HIDDEN, dtype=F32),
            whole(LOCALS, SLOTS, HIDDEN),
            whole(PAIRS, EXPERTS * TWICE, HIDDEN),
            whole(4, ROWS, WIDTH_B),
            whole(4, ROWS, WIDTH_B),
            dma(3), dma(5), dma(5), dma(2, 8), dma(2, 8), dma(2, 4, 2), dma(2, 4, 2),
            dma(2, 4, 1), dma(2, 4, 1), dma(2, 4, 4), dma(2, 4, 4), dma(5, 8), dma(5, 8),
            pltpu.SemaphoreType.REGULAR((4,)), pltpu.SemaphoreType.REGULAR,
            dma(5, 8), dma(5, 8), dma(2, 4, 4), dma(2, 4, 4), dma(2, 4, 2), dma(2, 4, 2),
            dma(2, 8), dma(2, 8),
        ],
        compiler_params=pltpu.CompilerParams(
            collective_id=0, has_side_effects=True, vmem_limit_bytes=VMEM_BYTES
        ),
        name="layer",
    )(hidden_in[0], norm_gain, router[0].T, routes[0].T, w_gate[0, 0], w_up[0, 0], w_down[0, 0])
    return out[None]


def solution(mesh):
    placed = (
        P("section", ("group", "local"), None),
        P("section", None),
        P("section", None, None),
        P("section", "group", None, "local"),
        P("section", "group", None, "local"),
        P("section", "group", "local", None),
        P("section", ("group", "local"), None),
    )
    return jax.shard_map(
        per_device,
        mesh=mesh,
        in_specs=placed,
        out_specs=P("section", ("group", "local"), None),
        check_vma=False,
    )
```

```python
import jax
import jax.numpy as jnp
from jax import lax
from jax.experimental import pallas as pl
from jax.experimental.pallas import tpu as pltpu
from jax.sharding import PartitionSpec as P

WIDTH = 7168
WIDTH_A = 3456
WIDTH_B = WIDTH - WIDTH_A
META = 128
QUARTER = 896
QUARTERS = ((0, 896), (896, 896), (1792, 896), (2688, 768))
PARTS = ((0, 1792), (1792, WIDTH_B - 1792))
WIDTH_BX = META + WIDTH_B
EXPERTS = 8
LOCALS = 8
SECTIONS = 4
ROWS = 64
CAP = 24
TWICE = 2 * CAP
SLOTS = EXPERTS * CAP
PAIRS = LOCALS // 2
HIDDEN = 256
TILE = 256
LANES = 128
VMEM_BYTES = 63 * 2**20

BF16 = jnp.bfloat16
F32 = jnp.float32


def wrap(value, count=8):
    return lax.rem(value + 2 * count, count)


def matmul(left, right):
    return jnp.dot(left, right, preferred_element_type=F32)


def lanes_at(start, size):
    return pl.ds(pl.multiple_of(start, LANES), size)


def sweep(width, part):
    @pl.loop(0, width // TILE)
    def _(tile):
        part(tile * TILE, TILE)

    if width % TILE:
        part(width // TILE * TILE, width % TILE)


def pair_at(pair):
    return pl.ds(pl.multiple_of(pair * TWICE, TWICE), TWICE)


def remote(src, dst, send, recv, device):
    return pltpu.make_async_remote_copy(
        src_ref=src, dst_ref=dst, send_sem=send, recv_sem=recv, device_id=device
    )


def peers_of(group):
    chip, core = group // 2, lax.rem(group, 2)
    out = []
    for index, (ahead, flip) in enumerate(((1, 0), (3, 0), (2, 0), (1, 1), (3, 1), (2, 1), (0, 1))):
        there = 1 - core if flip else core
        out.append((index, wrap(chip + ahead, 4) * 2 + there))
    return out


def hops_of(piece, pieces, way):
    first = piece < pieces // 2
    return 4 if first == (way == 0) else 3


def pairs_near_first(local):
    own = local // 2
    odd = lax.rem(local, 2)
    return [own, wrap(own + 2 * odd - 1, PAIRS), wrap(own - 2 * odd + 1, PAIRS), wrap(own + 2, PAIRS)]


def slot_masks(meta, expert_of, slot_of):
    out = []
    for choice in range(2):
        expert = meta[:, 2 * choice : 2 * choice + 1]
        slot = meta[:, 2 * choice + 1 : 2 * choice + 2]
        out.append((expert_of == expert) & (slot_of == slot))
    return out


def pair_masks(meta):
    shape = (2 * ROWS, EXPERTS * TWICE)
    column = lax.broadcasted_iota(jnp.int32, shape, 1)
    inside = lax.rem(column, TWICE)
    owner = lax.broadcasted_iota(jnp.int32, shape, 0) // ROWS
    slot = jnp.where(inside // CAP == owner, lax.rem(inside, CAP), -1)
    return slot_masks(meta, (column // TWICE).astype(F32), slot.astype(F32))


def gate_matrices(meta, gates):
    masks = pair_masks(meta)
    out = []
    for part in range(2):
        first, second = gates[:, part : 1 + part], gates[:, 2 + part : 3 + part]
        out.append((jnp.where(masks[0], first, 0.0) + jnp.where(masks[1], second, 0.0)).astype(BF16))
    return out


def layer_kernel(
    hid_ref, gain_ref, router_ref, routes_ref, wg_hbm, wu_hbm, wd_hbm, out_ref,
    wg, wu, wd, inc, scale_out, scale_in, na, disp, xa, za, zd, zb, zg, xs, xr, hacc, acta, actb, tu, td,
    w_sem, y_send, y_recv, xa_send, xa_recv, zb_send, zb_recv, zg_send, zg_recv, za_send, za_recv,
    xb_send, xb_recv, free_x, free_z,
    xc_send, xc_recv, zc_send, zc_recv, ze_send, ze_recv, xe_send, xe_recv,
):
    section = lax.axis_index("section")
    group, local = lax.axis_index("group"), lax.axis_index("local")
    ring = ({"local": wrap(local + 1)}, {"local": wrap(local - 1)})
    after = {"section": wrap(section + 1, SECTIONS)}
    sign = (1, -1)
    pairs = pairs_near_first(local)
    peers = peers_of(group)

    barrier = pltpu.get_barrier_semaphore()
    pl.semaphore_signal(barrier, inc=1, device_id={"section": wrap(section - 1, SECTIONS)})
    for way in range(2):
        pl.semaphore_signal(barrier, inc=1, device_id=ring[way])
    for _, other in peers:
        pl.semaphore_signal(barrier, inc=1, device_id={"group": other})
    loads = [
        pltpu.make_async_copy(hbm, here, w_sem.at[i])
        for i, (hbm, here) in enumerate(((wg_hbm, wg), (wu_hbm, wu), (wd_hbm, wd)))
    ]

    def start(copy, into):
        copy.start()
        into.append(copy)
        return copy


    chunks = tuple((WIDTH_A + begin, size) for begin, size in PARTS)
    chunks += ((0, 2 * QUARTER), (2 * QUARTER, WIDTH_A - 2 * QUARTER))
    shifts = []
    for number, (begin, size) in enumerate(chunks):
        view = pl.ds(begin, size)
        shifts.append(
            remote(hid_ref.at[:, view], inc.at[:, view], y_send.at[number], y_recv.at[number], after)
        )
    pl.semaphore_wait(barrier, 1 + 2 + EXPERTS - 1)
    shifts[0].start()
    squares = jnp.zeros((ROWS, 1), F32)
    for begin, size in chunks:
        values = hid_ref[:, pl.ds(begin, size)].astype(F32)
        squares = squares + jnp.sum(values * values, axis=-1, keepdims=True)
    scale_out[...] = jnp.broadcast_to(lax.rsqrt(squares / WIDTH + 1e-06), (ROWS, LANES))
    scale_copy = remote(scale_out, scale_in, y_send.at[4], y_recv.at[4], after)
    scale_copy.start()
    shifts[1].start()
    for load in loads:
        load.start()

    square = (ROWS, ROWS)
    down, across = lax.broadcasted_iota(jnp.int32, square, 0), lax.broadcasted_iota(jnp.int32, square, 1)
    lane = lax.broadcasted_iota(jnp.int32, (ROWS, META), 1)
    experts = []
    for choice in range(2):
        row = jnp.broadcast_to(routes_ref[choice : choice + 1, :].astype(F32), square)
        experts.append(jnp.sum(jnp.where(down == across, row, 0.0), axis=1, keepdims=True))
    named = [expert == lane.astype(F32) for expert in experts]
    counts = (named[0].astype(F32) + named[1].astype(F32)).astype(BF16)
    before = matmul((down > across).astype(F32).astype(BF16), counts)
    meta = jnp.zeros((ROWS, META), F32)
    for choice in range(2):
        slot = jnp.sum(jnp.where(named[choice], before, 0.0), axis=1, keepdims=True)
        meta = jnp.where(lane == 2 * choice, experts[choice], meta)
        meta = jnp.where(lane == 2 * choice + 1, slot, meta)

    column = lax.broadcasted_iota(jnp.int32, (ROWS, EXPERTS * 32), 1)
    masks = slot_masks(meta, (column // 32).astype(F32), lax.rem(column, 32).astype(F32))
    chosen = (masks[0] | masks[1]).astype(F32)
    chosen = jnp.transpose(jnp.concatenate([chosen, jnp.zeros_like(chosen)], axis=0))
    chosen = chosen.reshape(EXPERTS, 32, 2 * ROWS)[:, :CAP].reshape(SLOTS, 2 * ROWS)
    chosen = chosen[:, :ROWS].astype(BF16)

    def normed_chunk(number):
        shifts[number].wait_recv()
        if number + 2 < len(shifts):
            shifts[number].wait_send()
            shifts[number + 2].start()
        if number == 0:
            scale_copy.wait_recv()
        view = pl.ds(*chunks[number])
        values = inc[:, view].astype(F32) * scale_in[:, :1]
        normed = (values * gain_ref[:, view].astype(F32)).astype(BF16)
        logits = lax.dot_general(
            normed, router_ref[:, view], (((1,), (1,)), ((), ())), preferred_element_type=F32
        )
        return normed, logits

    def view_a(block, piece):
        return za.at[block, :, pl.ds(*QUARTERS[piece])]

    def view_b(block, piece):
        begin, size = PARTS[piece]
        return zb.at[block, :, pl.ds(META + begin, size) if piece else pl.ds(0, META + size)]

    def view_g(block, piece):
        return zg.at[block]

    sent_a, sent_b = [], []
    ring_a = (view_a, 4, za_send, za_recv, sent_a)
    ring_b = (view_b, 2, zb_send, zb_recv, sent_b)
    ring_g = (view_g, 2, zg_send, zg_recv, sent_b)

    def gather_copy(kind, way, hop, piece):
        view, _, sends, recvs, _ = kind
        there = view(wrap(local - sign[way] * (hop - 1)), piece)
        return remote(
            there, there, sends.at[way, hop - 1, piece], recvs.at[way, hop - 1, piece], ring[way]
        )

    def gather_open(kind, pieces):
        for piece in pieces:
            for way in range(2):
                start(gather_copy(kind, way, 1, piece), kind[4])

    def gather_step(kind, hop, pieces):
        for piece in pieces:
            for way in range(2):
                hops = hops_of(piece, kind[1], way)
                if hop <= hops:
                    gather_copy(kind, way, hop, piece).wait_recv()
                if hop < hops:
                    start(gather_copy(kind, way, hop + 1, piece), kind[4])

    xa_copies = ([], [])

    def by_quarters(half, part):
        few = QUARTERS[2 * half + 1][1] // LANES

        @pl.loop(0, few)
        def _(tile):
            part(tile * LANES, 2)

        if few * LANES < QUARTER:
            part(few * LANES, 1)

    def stacked(parts):
        if len(parts) == 1:
            parts = parts + [jnp.zeros_like(parts[0])]
        return jnp.concatenate(parts, axis=1).astype(BF16)

    def exchange(half, sends, recvs, copies):
        for step, other in peers:
            copy = remote(
                disp.at[half, other], xa.at[half, group], sends.at[half, step], recvs.at[half, step],
                {"group": other},
            )
            start(copy, copies)
        xa[half, group] = disp[half, group]

    def spread(half, normed):
        na[:, : normed.shape[1]] = normed

        def part(begin, quarters):
            parts = [
                matmul(chosen, na[:, lanes_at(quarter * QUARTER + begin, LANES)])
                for quarter in range(quarters)
            ]
            parts = [rows.reshape(EXPERTS, CAP, LANES) for rows in parts]
            disp[half, :, :, lanes_at(begin, LANES)] = stacked(parts)

        by_quarters(half, part)
        exchange(half, xa_send, xa_recv, xa_copies[half])

    def compact(half):
        for copy in xa_copies[half]:
            copy.wait_recv()

        def part(begin, quarters):
            rows = xa[half, :, :, lanes_at(begin, LANES)].astype(F32)
            for quarter in range(quarters):
                some = rows[:, quarter * CAP : (quarter + 1) * CAP].reshape(SLOTS, LANES)
                columns = lanes_at((2 * half + quarter) * QUARTER + begin, LANES)
                za[local, :, columns] = some.astype(BF16)

        by_quarters(half, part)
        gather_open(ring_a, (2 * half, 2 * half + 1))

    def select(pair, place, begin, width):
        both = zb[pl.ds(2 * pair, 2), :, :META].reshape(2 * ROWS, META).astype(F32)
        masks = pair_masks(both)
        selector = jnp.transpose((masks[0] | masks[1]).astype(F32)).astype(BF16)

        def part(start, size):
            rows = zb[pl.ds(2 * pair, 2), :, lanes_at(META + begin + start, size)]
            out = matmul(selector, rows.reshape(2 * ROWS, size)).astype(BF16)
            xs[place, :, :, lanes_at(begin + start, size)] = out.reshape(EXPERTS, TWICE, size)

        sweep(width, part)

    def send_pair(pair, place, sends, recvs, begin=0, width=WIDTH_B):
        copies = []
        columns = pl.ds(begin, width)
        for step, other in peers:
            copy = remote(
                xs.at[place, other, :, columns], xr.at[group, pair_at(pair), columns],
                sends.at[step], recvs.at[step], {"group": other},
            )
            start(copy, copies)
        xr[group, pair_at(pair), columns] = xs[place, group, :, columns]
        return copies

    xb_copies = [[], [], [], []]

    def give_pair(order, begin=0, width=WIDTH_B):
        if order == 3:
            for copy in xb_copies[0]:
                copy.wait_send()
        select(pairs[order], order % 3, begin, width)
        row = order if begin == 0 else 4
        xb_copies[order] += send_pair(
            pairs[order], order % 3, xb_send.at[row], xb_recv.at[row], begin, width
        )

    normed, logits = normed_chunk(0)
    zb[local, :, :META] = meta.astype(BF16)
    zb[local, :, META : META + PARTS[1][0]] = normed
    gather_open(ring_b, (0,))
    normed, more = normed_chunk(1)
    logits = logits + more
    zb[local, :, META + PARTS[1][0] :] = normed
    gather_open(ring_b, (1,))
    gather_step(ring_b, 1, (0,))
    give_pair(0, *PARTS[0])
    normed, more = normed_chunk(2)
    logits = logits + more
    spread(0, normed)
    gather_step(ring_b, 1, (1,))
    give_pair(0, *PARTS[1])
    gather_step(ring_b, 2, (0,))
    normed, more = normed_chunk(3)
    spread(1, normed)
    affinity = jax.nn.sigmoid(logits + more)
    expert = lax.broadcasted_iota(jnp.int32, (ROWS, EXPERTS), 1).astype(F32)
    picked = [
        jnp.sum(jnp.where(experts[choice] == expert, affinity, 0.0), axis=1, keepdims=True)
        for choice in range(2)
    ]
    gates = jnp.zeros((ROWS, META), F32)
    for choice in range(2):
        gate = 2.5 * picked[choice] / (picked[0] + picked[1])
        high = gate.astype(BF16).astype(F32)
        gates = jnp.where(lane == 2 * choice, high, gates)
        gates = jnp.where(lane == 2 * choice + 1, gate - high, gates)
    zg[local] = gates.astype(BF16)
    gather_open(ring_g, (0,))
    gather_step(ring_b, 2, (1,))
    give_pair(1)
    gather_step(ring_b, 3, (0,))
    compact(0)
    gather_step(ring_b, 3, (1,))
    compact(1)
    give_pair(2)
    gather_step(ring_b, 4, (0,))
    gather_step(ring_b, 4, (1,))
    gather_step(ring_g, 1, (0,))

    def add_a(block):
        block = wrap(block)
        rows = za[block]
        for half, weights in enumerate((wg, wu)):
            out = matmul(rows, weights[:WIDTH_A, :]).reshape(EXPERTS, CAP, HIDDEN)
            hacc[block, :, :, half * HIDDEN : (half + 1) * HIDDEN] = out

    def take(hop):
        count = 1 if hop in (0, 4) else 2

        @pl.loop(0, count)
        def _(i):
            add_a(local - hop + 2 * hop * i)

    def finish(order):
        pair = pairs[order]
        rows = xr[:, pair_at(pair), :].reshape(EXPERTS * TWICE, WIDTH_B)
        parts = []
        for half, weights in enumerate((wg, wu)):
            out = matmul(rows, weights[WIDTH_A:, :]).reshape(EXPERTS, 2, CAP, HIDDEN)
            done = [
                hacc[2 * pair + block, :, :, half * HIDDEN : (half + 1) * HIDDEN] + out[:, block]
                for block in range(2)
            ]
            parts.append(done)
        active = [jax.nn.silu(parts[0][block]) * parts[1][block] for block in range(2)]
        for block in range(2):
            acta[2 * pair + block] = active[block].reshape(SLOTS, HIDDEN).astype(BF16)
        both = jnp.concatenate(active, axis=1)
        actb[pair] = both.reshape(EXPERTS * TWICE, HIDDEN).astype(BF16)
        for _, other in peers:
            pl.semaphore_signal(free_x.at[order], inc=1, device_id={"group": other})

    def product_b(pair, place):
        def part(begin, size):
            out = matmul(actb[pair], wd[:, lanes_at(WIDTH_A + begin, size)]).astype(BF16)
            xs[place, :, :, lanes_at(begin, size)] = out.reshape(EXPERTS, TWICE, size)

        sweep(WIDTH_B, part)

    xc_copies = {}

    def return_pair(order, place, blocking, parts=((0, WIDTH_B),)):
        if blocking is not None:
            for copy in blocking:
                copy.wait_send()
            product_b(pairs[order], place)
        pl.semaphore_wait(free_x.at[order], EXPERTS - 1)
        xc_copies[order] = []
        for number, (begin, width) in enumerate(parts):
            row = 4 if number else order
            copies = send_pair(
                pairs[order], place, xc_send.at[row], xc_recv.at[row], begin, width
            )
            xc_copies[order].append(copies)

    loads[0].wait()
    loads[1].wait()
    take(0)
    for hop in range(1, 5):
        if hop == 4:
            loads[2].wait()
            for copy in xb_copies[1]:
                copy.wait_send()
            product_b(pairs[1], 1)
        gather_step(ring_a, hop, range(4))
        if hop < 4:
            gather_step(ring_g, hop + 1, (0,))
        take(hop)
        if hop == 4:
            for copy in sent_a:
                copy.wait_send()
            for way in range(2):
                pl.semaphore_signal(free_z, inc=1, device_id=ring[way])
        for copy in xb_copies[hop - 1]:
            copy.wait_recv()
        if hop == 4:
            return_pair(1, 1, None)
        finish(hop - 1)
        if hop == 1:
            give_pair(3)


    sent_c = []

    def product_a(block, piece, fresh):
        block = wrap(block)

        base, width = QUARTERS[piece]

        def part(begin, size):
            columns = lanes_at(base + begin, size)
            out = matmul(acta[block], wd[:, columns])
            if not fresh:
                out = out + za[block, :, columns].astype(F32)
            za[block, :, columns] = out.astype(BF16)

        sweep(width, part)

    def sum_copy_a(way, hop, piece):
        block = wrap(local + sign[way] * (5 - hop))
        columns = pl.ds(*QUARTERS[piece])
        lands = zd.at[:, columns] if (way, hop) == (1, 4) else za.at[block, :, columns]
        return remote(
            za.at[block, :, columns], lands,
            zc_send.at[way, hop - 1, piece], zc_recv.at[way, hop - 1, piece], ring[way],
        )

    def sum_open_a(hop):
        for piece in range(4):
            for way in range(2):
                if hop == 5 - hops_of(piece, 4, way):
                    product_a(local + sign[way] * (5 - hop), piece, True)
                    start(sum_copy_a(way, hop, piece), sent_c)

    def sum_step_a(hop):
        for piece in range(4):
            for way in range(2):
                if hop > 5 - hops_of(piece, 4, way):
                    sum_copy_a(way, hop - 1, piece).wait_recv()
                    product_a(local + sign[way] * (5 - hop), piece, False)
                    start(sum_copy_a(way, hop, piece), sent_c)

    def sum_copy_b(way, hop, piece):
        block = wrap(local + sign[way] * (5 - hop))
        begin, size = PARTS[piece]
        return remote(
            zb.at[block, :, pl.ds(META + begin, size)],
            (tu, td)[way].at[hop - 1, :, pl.ds(begin, size)],
            ze_send.at[way, hop - 1, piece], ze_recv.at[way, hop - 1, piece], ring[way],
        )

    def sum_step_b(hop, pieces=(0, 1)):
        for piece in pieces:
            for way in range(2):
                opens = 5 - hops_of(piece, 2, way)
                if hop > opens:
                    sum_copy_b(way, hop - 1, piece).wait_recv()
                    block = wrap(local + sign[way] * (5 - hop))
                    begin, size = PARTS[piece]
                    came = (tu, td)[way][hop - 2, :, pl.ds(begin, size)]
                    zb[block, :, pl.ds(META + begin, size)] += came
                if hop >= opens:
                    start(sum_copy_b(way, hop, piece), sent_c)

    def mix_pair(order, number=0, base=0, width=WIDTH_B):
        pair = pairs[order]
        for copy in xc_copies[order][number]:
            copy.wait_recv()
        both = zb[pl.ds(2 * pair, 2), :, :META].reshape(2 * ROWS, META).astype(F32)
        weights = zg[pl.ds(2 * pair, 2)].reshape(2 * ROWS, META).astype(F32)
        high, low = gate_matrices(both, weights)

        def part(begin, size):
            rows = xr[:, pair_at(pair), lanes_at(base + begin, size)].reshape(EXPERTS * TWICE, size)
            mixed = matmul(high, rows) + matmul(low, rows)
            mixed = mixed.astype(BF16).reshape(2, ROWS, size)
            zb[pl.ds(2 * pair, 2), :, lanes_at(META + base + begin, size)] = mixed

        sweep(width, part)

    pl.semaphore_wait(free_z, 2)
    sum_open_a(1)
    return_pair(3, 2, xb_copies[2])
    sum_open_a(2)
    for copy in sent_b + xa_copies[0] + xa_copies[1]:
        copy.wait_send()
    sum_step_a(2)
    return_pair(2, 0, xb_copies[3])
    sum_step_a(3)
    return_pair(0, 1, xc_copies[1][0], PARTS)
    mix_pair(3)
    sum_step_b(1)
    sum_step_a(4)
    mix_pair(2)
    sum_step_b(2)
    mix_pair(1)

    xe_copies = ([], [])

    def total_a(columns):
        total = matmul(acta[local], wd[:, columns])
        total = total + za[local, :, columns].astype(F32) + zd[:, columns].astype(F32)
        return total.reshape(EXPERTS, CAP, LANES)

    for half in range(2):
        for piece in (2 * half, 2 * half + 1):
            for way in range(2):
                sum_copy_a(way, 4, piece).wait_recv()

        def part(begin, quarters, half=half):
            parts = [
                total_a(lanes_at((2 * half + quarter) * QUARTER + begin, LANES))
                for quarter in range(quarters)
            ]
            disp[half, :, :, lanes_at(begin, LANES)] = stacked(parts)

        by_quarters(half, part)
        exchange(half, xe_send, xe_recv, xe_copies[half])
    sum_step_b(3)
    for piece in range(2):
        mix_pair(0, piece, *PARTS[piece])
        sum_step_b(4, (piece,))

    own, weights = zb[local, :, :META].astype(F32), zg[local].astype(F32)
    high, low = gate_matrices(
        jnp.concatenate([own, own], axis=0), jnp.concatenate([weights, weights], axis=0)
    )
    for half in range(2):
        for copy in xe_copies[half]:
            copy.wait_recv()

        def part(begin, quarters, half=half):
            rows = xa[half, :, :, lanes_at(begin, LANES)].reshape(EXPERTS * TWICE, LANES)
            mixed = matmul(high, rows) + matmul(low, rows)
            for quarter in range(quarters):
                columns = lanes_at((2 * half + quarter) * QUARTER + begin, LANES)
                some = mixed[quarter * ROWS : (quarter + 1) * ROWS]
                out_ref[:, columns] = (inc[:, columns].astype(F32) + some).astype(BF16)

        by_quarters(half, part)

    for piece in range(2):
        for way in range(2):
            sum_copy_b(way, 4, piece).wait_recv()

    def close(begin, size):
        columns, places = lanes_at(begin, size), lanes_at(WIDTH_A + begin, size)
        mixed = zb[local, :, lanes_at(META + begin, size)].astype(F32)
        mixed = mixed + tu[3, :, columns].astype(F32) + td[3, :, columns].astype(F32)
        out_ref[:, places] = (inc[:, places].astype(F32) + mixed).astype(BF16)

    sweep(WIDTH_B, close)
    scale_copy.wait_send()
    for copy in shifts[2:] + sent_c + xe_copies[0] + xe_copies[1]:
        copy.wait_send()
    for copies in xc_copies[3] + xc_copies[2] + xc_copies[0]:
        for copy in copies:
            copy.wait_send()


def whole(*shape, dtype=BF16):
    return pltpu.VMEM(shape, dtype)


def dma(*shape):
    return pltpu.SemaphoreType.DMA(shape)


def per_device(hidden_in, norm_gain, router, w_gate, w_up, w_down, routes):
    vmem = pl.BlockSpec(memory_space=pltpu.VMEM)
    anywhere = pl.BlockSpec(memory_space=pl.ANY)
    out = pl.pallas_call(
        layer_kernel,
        out_shape=jax.ShapeDtypeStruct((ROWS, WIDTH), BF16),
        in_specs=[vmem] * 4 + [anywhere] * 3,
        out_specs=vmem,
        scratch_shapes=[
            whole(WIDTH, HIDDEN),
            whole(WIDTH, HIDDEN),
            whole(HIDDEN, WIDTH),
            whole(ROWS, WIDTH),
            whole(ROWS, LANES, dtype=F32),
            whole(ROWS, LANES, dtype=F32),
            whole(ROWS, 2 * QUARTER),
            whole(2, EXPERTS, TWICE, QUARTER),
            whole(2, EXPERTS, TWICE, QUARTER),
            whole(LOCALS, SLOTS, WIDTH_A),
            whole(SLOTS, WIDTH_A),
            whole(LOCALS, ROWS, WIDTH_BX),
            whole(LOCALS, ROWS, META),
            whole(3, EXPERTS, TWICE, WIDTH_B),
            whole(EXPERTS, SLOTS, WIDTH_B),
            whole(LOCALS, EXPERTS, CAP, 2 * HIDDEN, dtype=F32),
            whole(LOCALS, SLOTS, HIDDEN),
            whole(PAIRS, EXPERTS * TWICE, HIDDEN),
            whole(4, ROWS, WIDTH_B),
            whole(4, ROWS, WIDTH_B),
            dma(3), dma(5), dma(5), dma(2, 8), dma(2, 8), dma(2, 4, 2), dma(2, 4, 2),
            dma(2, 4, 1), dma(2, 4, 1), dma(2, 4, 4), dma(2, 4, 4), dma(5, 8), dma(5, 8),
            pltpu.SemaphoreType.REGULAR((4,)), pltpu.SemaphoreType.REGULAR,
            dma(5, 8), dma(5, 8), dma(2, 4, 4), dma(2, 4, 4), dma(2, 4, 2), dma(2, 4, 2),
            dma(2, 8), dma(2, 8),
        ],
        compiler_params=pltpu.CompilerParams(
            collective_id=0, has_side_effects=True, vmem_limit_bytes=VMEM_BYTES
        ),
        name="layer",
    )(hidden_in[0], norm_gain, router[0].T, routes[0].T, w_gate[0, 0], w_up[0, 0], w_down[0, 0])
    return out[None]


def solution(mesh):
    placed = (
        P("section", ("group", "local"), None),
        P("section", None),
        P("section", None, None),
        P("section", "group", None, "local"),
        P("section", "group", None, "local"),
        P("section", "group", "local", None),
        P("section", ("group", "local"), None),
    )
    return jax.shard_map(
        per_device,
        mesh=mesh,
        in_specs=placed,
        out_specs=P("section", ("group", "local"), None),
        check_vma=False,
    )
```
